512 devices in a mesh: ctx: 64 (over y_hi, z, x), head: 8 (over y_lo, core).
Axes of the slice: x: 4, y: 8 (y_hi: 2, y_lo: 4; y = y_hi * 4 + y_lo), z: 8, core: 2. Of those that a mesh axis runs over, the one named last changes fastest.
Arguments:
- queries: bfloat16 [8, 8192, 128], P('head', 'ctx'), may hold values from -32 to 32
- keys: bfloat16 [8192, 128], P('ctx'), may hold values from -6 to 6
- values: bfloat16 [8192, 128], P('ctx'), may hold values from -6 to 6
- grad_out: bfloat16 [8, 8192, 128], P('head', 'ctx'), may hold values from -6 to 6
- order: int32 [128], replicated, may hold values from 0 to 127, each once
- segment: int32 [8192], replicated, may hold values from 0 to 5, as said below
Outputs:
- grad_queries: bfloat16 [8, 8192, 128], P('head', 'ctx')
- grad_keys: bfloat16 [8192, 128], P('ctx')
- grad_values: bfloat16 [8192, 128], P('ctx')
The draws below stay inside these ranges and needn't reach their ends.
Inputs may be any that keep to these rules, and one draw needn't show every extreme that they name: `order`: a permutation of the 128 block numbers. `segment`: nondecreasing along positions; every document starts at an even position; ids 0 and 5 both occur.
All inputs are finite; a program needn't handle non-finite values.
Results may differ from the reference program's by a relative error of at most 0.0055.
Values may be sent and summed in bfloat16 or wider, within the bound.
A program may use at most 64 MiB of HBM per device.

```python
import math
import jax
import jax.numpy as jnp
from jax import lax

HEADS = 8
HD = 128
DOCS = 6
SPAN = 64
SPANS = 128
TOKENS = 8192


def draw_keys(key, part):
    key = jax.random.fold_in(key, 1)
    drawn = jnp.clip(jax.random.normal(key, (TOKENS, HD), jnp.float32), -6.0, 6.0)
    return drawn.astype(jnp.bfloat16)


def draw_queries(key, part):
    key = jax.random.fold_in(key, 2)
    drawn = jnp.clip(jax.random.normal(key, (HEADS, TOKENS, HD), jnp.float32), -6.0, 6.0)
    return drawn.astype(jnp.bfloat16)


def draw_segment(key, part):
    key = jax.random.fold_in(key, 5)
    picks = jax.random.permutation(key, TOKENS // 2 - 1)[:DOCS - 1]
    bounds = 2 * (picks + 1)
    position = jnp.arange(TOKENS, dtype=jnp.int32)
    return jnp.sum((position[:, None] >= bounds[None, :]).astype(jnp.int32), axis=1).astype(jnp.int32)


def block_scale(own_key, shape, cuts, smallest, top_value):
    def one(dim, parts):
        steps = jax.random.uniform(jax.random.fold_in(jax.random.fold_in(own_key, 6), dim), (parts,), jnp.float32, smallest / len(cuts), top_value / len(cuts))
        return jnp.repeat(jnp.exp(steps), shape[dim] // parts).reshape((-1,) + (1,) * (len(shape) - dim - 1))

    gain = one(*cuts[0])
    for cut in cuts[1:]:
        gain = gain * one(*cut)
    return gain


def bell_draw(stream_key, dims, spread, limit, pieces=(), kind=jnp.bfloat16):
    level = block_scale(stream_key, dims, pieces, -0.22, 0.18) if pieces else 1.0
    entries = jax.random.normal(stream_key, dims, jnp.float32) * spread * level
    return jnp.minimum(jnp.maximum(entries, -limit), limit).astype(kind)


def setup_inputs(seed: int = 0) -> dict:
    seeds = jax.random.split(jax.random.key(seed), 7)
    queries = draw_queries(jax.random.fold_in(seeds[6], 71), 0)
    keys = draw_keys(jax.random.fold_in(seeds[6], 71), 0)
    values = bell_draw(seeds[2], (TOKENS, HD), 1.0, 6.0, ((0, 64),))
    grad_out = bell_draw(seeds[3], (HEADS, TOKENS, HD), 1.0, 6.0, ((0, 8), (1, 64)))
    order = jax.random.permutation(seeds[4], SPANS).astype(jnp.int32)
    segment = draw_segment(jax.random.fold_in(seeds[6], 71), 0)
    return dict(queries=queries, keys=keys, values=values, grad_out=grad_out, order=order, segment=segment)


def block_of(total):
    return max((d for d in range(1, min(total, 512) + 1) if total % d == 0))

def reference(queries, keys, values, grad_out, order, segment):
    rows = jnp.arange(TOKENS, dtype=jnp.int32)
    position = (order[rows // SPAN] * SPAN + rows % SPAN).astype(jnp.int32)
    doc = segment[position]
    scale = 1.0 / math.sqrt(HD)
    size = block_of(TOKENS)
    count = TOKENS // size

    def step(carry, index):
        grad_k, grad_v = carry
        head = (index // count).astype(jnp.int32)
        start = (index % count * size).astype(jnp.int32)
        head_q = lax.dynamic_index_in_dim(queries, head, 0, keepdims=False)
        head_go = lax.dynamic_index_in_dim(grad_out, head, 0, keepdims=False)
        block_q = lax.dynamic_slice_in_dim(head_q, start, size, 0)
        block_go = lax.dynamic_slice_in_dim(head_go, start, size, 0)
        query_pos = lax.dynamic_slice_in_dim(position, start, size, 0)
        query_doc = lax.dynamic_slice_in_dim(doc, start, size, 0)
        allowed = (position[None, :] <= query_pos[:, None]) & (doc[None, :] == query_doc[:, None])
        scores = jnp.dot(block_q, keys.T, preferred_element_type=jnp.float32) * scale
        masked = jnp.where(allowed, scores, jnp.float32(-1e+30))
        peak = lax.optimization_barrier(jnp.max(masked, axis=1))
        lse = peak + jnp.log(lax.optimization_barrier(jnp.sum(jnp.where(allowed, jnp.exp(masked - peak[:, None]), 0.0), axis=1)))
        probs = jnp.where(allowed, jnp.exp(scores - lse[:, None]), 0.0)
        dprobs = jnp.dot(block_go, values.T, preferred_element_type=jnp.float32)
        delta = lax.optimization_barrier(jnp.sum(probs * dprobs, axis=1))
        dscores = (probs * (dprobs - delta[:, None]) * scale).astype(jnp.bfloat16)
        grad_q = jnp.dot(dscores, keys, preferred_element_type=jnp.float32).astype(jnp.bfloat16)
        grad_k = grad_k + jnp.dot(dscores.T, block_q, preferred_element_type=jnp.float32)
        grad_v = grad_v + jnp.dot(probs.astype(jnp.bfloat16).T, block_go, preferred_element_type=jnp.float32)
        return ((grad_k, grad_v), grad_q)
    zeros = jnp.zeros((TOKENS, HD), jnp.float32)
    (grad_k, grad_v), blocks = lax.scan(step, (zeros, zeros), jnp.arange(HEADS * count, dtype=jnp.int32))
    grad_queries = blocks.reshape(HEADS, TOKENS, HD)
    return (grad_queries, grad_k.astype(jnp.bfloat16), grad_v.astype(jnp.bfloat16))
```

```python
import functools
import math

import jax
import jax.numpy as jnp
from jax import lax
from jax.experimental import pallas as pl
from jax.experimental.pallas import tpu as pltpu
from jax.sharding import PartitionSpec as P

YH, Z, X, YL, CORES = 2, 8, 4, 4, 2
DOCS = 6
SPAN = 64
ROWS = 2 * SPAN
WIDTH = 128
TILE = 1024
LANES = 256
PARTS = TILE // LANES
CHUNK = 128
NEGATIVE = -1e30
FLOOR = -1e20
MESH = pl.DeviceIdType.MESH
SCALE = 1.0 / math.sqrt(WIDTH)
LOG2E = 1.4426950408889634
NT = (((1,), (1,)), ((), ()))
TN = (((0,), (0,)), ((), ()))


def device(yh, z, x, yl, c):
    return {"ctx": yh * (Z * X) + z * X + x, "head": yl * CORES + c}


def kernel(
    order, segment, q_in, k_in, v_in, go_in, dq_out, dk_out, dv_out,
    qbuf, kv, kbuf, scores, dprobs, pair, peaks, lows, highs, stats,
    give, take, total, gathered, pieces, dq_part, dq_took,
    local_sem, send_sem, recv_sem, swap_sem,
):
    i, h = lax.axis_index("ctx"), lax.axis_index("head")
    yh, z, x = lax.div(i, Z * X), lax.rem(lax.div(i, X), Z), lax.rem(i, X)
    yl, c = lax.div(h, CORES), lax.rem(h, CORES)
    yp, yj = lax.rem(yl, 2), lax.div(yl, 2)
    own = yp * X + x
    sibling = device(yh, z, x, yl, 1 - c)

    def query_peer(n):
        tx = lax.rem(x + lax.rem(n, X), X)
        tp = lax.rem(yp + lax.div(n, X), 2)
        return device(yh, z, tx, yj * 2 + tp, c), tp * X + tx

    def near_peer(n):
        return device(yh, lax.rem(z + n, Z), x, yl, c)

    def far_peer(n):
        return device(1 - yh, lax.rem(z + n, Z), x, YL - 1 - yl, c)

    def owner(n):
        g, dz, jj = lax.div(n, 16), lax.rem(lax.div(n, 2), Z), lax.rem(n, 2)
        tj = lax.rem(yj + jj, 2)
        where = device(lax.rem(yh + g, 2), lax.rem(z + Z - dz, Z), x, tj * 2 + yp, c)
        return where, lax.div(n, 2) * SPAN + tj * 32

    def head_peer(n):
        return device(yh, z, x, lax.rem(yl + lax.div(n, 2), YL), lax.rem(c + n, 2))

    def remote(src, dst, send, recv, where):
        return pltpu.make_async_remote_copy(
            src_ref=src, dst_ref=dst, send_sem=send, recv_sem=recv,
            device_id=where, device_id_type=MESH,
        )

    def wait_for(ref, sem):
        pltpu.make_async_copy(ref, ref, sem).wait()

    def loop(first, last, body):
        def step(n, carry):
            body(n)
            return carry

        lax.fori_loop(first, last, step, 0)

    mine = pl.ds(pl.multiple_of(own * ROWS, ROWS), ROWS)
    loads = [
        pltpu.make_async_copy(k_in, kv.at[0], local_sem.at[0]),
        pltpu.make_async_copy(v_in, kv.at[1], local_sem.at[1]),
        pltpu.make_async_copy(q_in.at[0], qbuf.at[0, mine], local_sem.at[2]),
        pltpu.make_async_copy(go_in.at[0], qbuf.at[1, mine], local_sem.at[3]),
    ]
    for copy in loads:
        copy.start()

    barrier = pltpu.get_barrier_semaphore()

    def greet(where):
        pl.semaphore_signal(barrier, inc=1, device_id=where, device_id_type=MESH)

    loop(1, 32, lambda n: greet(owner(n)[0]))
    loop(0, 8, lambda n: greet(far_peer(n)))
    loop(1, 8, lambda n: greet(query_peer(n)[0]))
    loop(1, 8, lambda n: greet(head_peer(n)))

    for copy in loads:
        copy.wait()
    half = pl.ds(pl.multiple_of(yp * SPAN, SPAN), SPAN)
    other = pl.ds(pl.multiple_of((1 - yp) * SPAN, SPAN), SPAN)
    kbuf[:, :SPAN] = kv[:, half]

    pl.semaphore_wait(barrier, 31 + 8 + 7 + 7)

    def send_far(n):
        rows = pl.ds(pl.multiple_of(512 + n * SPAN, SPAN), SPAN)
        remote(kv.at[c, other], kbuf.at[c, rows], send_sem.at[0], recv_sem.at[1], far_peer(n)).start()

    def send_near(n):
        rows = pl.ds(pl.multiple_of(n * SPAN, SPAN), SPAN)
        remote(kv.at[c, half], kbuf.at[c, rows], send_sem.at[0], recv_sem.at[0], near_peer(n)).start()

    def send_query(n):
        remote(qbuf.at[:, mine], qbuf.at[:, mine], send_sem.at[1], recv_sem.at[2], query_peer(n)[0]).start()

    loop(0, 8, send_far)
    loop(1, 8, send_near)
    loop(1, 8, send_query)

    docs = segment[...]
    starts = [
        jnp.sum((docs < d).astype(jnp.int32), axis=(0, 1), keepdims=True) for d in range(1, DOCS)
    ]
    lane = lax.broadcasted_iota(jnp.int32, (8, ROWS), 1)
    for s in range(X):
        ctx = yh * (Z * X) + z * X + s
        first, second = order[2 * ctx], order[2 * ctx + 1]
        place = jnp.where(lane < SPAN, first * SPAN + lane, second * SPAN + lane - SPAN)
        low = jnp.zeros_like(place)
        for start in starts:
            low = jnp.maximum(low, jnp.where(start <= place, start, 0))
        for t in (s, s + X):
            lows[t // 2, :, (t % 2) * ROWS : (t % 2 + 1) * ROWS] = low
            highs[t // 2, :, (t % 2) * ROWS : (t % 2 + 1) * ROWS] = place

    wait_for(kbuf.at[0, pl.ds(SPAN, 448)], recv_sem.at[0])
    near = kbuf.at[c, pl.ds(SPAN, 448)]
    swap_near = remote(near, near, swap_sem.at[0], swap_sem.at[1], sibling)
    swap_near.start()
    wait_for(kbuf.at[0, pl.ds(512, 512)], recv_sem.at[1])
    far = kbuf.at[c, pl.ds(512, 512)]
    swap_far = remote(far, far, swap_sem.at[2], swap_sem.at[3], sibling)
    swap_far.start()
    wait_for(qbuf.at[:, pl.ds(ROWS, 7 * ROWS)], recv_sem.at[2])

    row = lax.broadcasted_iota(jnp.int32, (SPAN, LANES), 0)

    def product(g, t):
        rows = pl.ds(pl.multiple_of(t * LANES, LANES), LANES)
        low, high = lows[t, 0:1, :], highs[t, 0:1, :]
        s = lax.dot_general(
            kbuf[0, g * 512 : g * 512 + 512], qbuf[0, rows], NT, preferred_element_type=jnp.float32
        )
        peak = None if g == 0 else peaks[t]
        for n in range(8):
            ctx = lax.rem(yh + g, 2) * (Z * X) + lax.rem(z + Z - n, Z) * X + x
            place = order[2 * ctx + yp] * SPAN + row
            masked = jnp.where(
                (place >= low) & (place <= high), s[n * SPAN : n * SPAN + SPAN], NEGATIVE
            )
            scores[t, g * 512 + n * SPAN : g * 512 + n * SPAN + SPAN] = masked
            top = jnp.max(masked.reshape(SPAN // 8, 8, LANES), axis=0)
            peak = top if peak is None else jnp.maximum(peak, top)
        peaks[t] = peak
        dprobs[t, g * 512 : g * 512 + 512] = lax.dot_general(
            kbuf[1, g * 512 : g * 512 + 512], qbuf[1, rows], NT, preferred_element_type=jnp.float32
        )

    swap_near.wait_recv()
    loop(0, PARTS, functools.partial(product, 0))
    swap_far.wait_recv()
    loop(0, PARTS, functools.partial(product, 1))

    def summed(a):
        return jnp.sum(a.reshape(CHUNK // 8, 8, LANES), axis=0)

    def weigh(t):
        peak = jnp.maximum(jnp.max(peaks[t], axis=0, keepdims=True), FLOOR)

        def step(r, carry):
            rows = pl.ds(pl.multiple_of(r * CHUNK, CHUNK), CHUNK)
            expo = jnp.exp2((scores[t, rows] - peak) * (SCALE * LOG2E))
            scores[t, rows] = expo
            return carry[0] + summed(expo), carry[1] + summed(expo * dprobs[t, rows])

        zero = jnp.zeros((8, LANES), jnp.float32)
        mass, weighted = lax.fori_loop(0, TILE // CHUNK, step, (zero, zero))
        mass = jnp.maximum(jnp.sum(mass, axis=0, keepdims=True), 1e-30)
        weighted = jnp.sum(weighted, axis=0, keepdims=True)
        peaks[t] = jnp.broadcast_to(peak * (SCALE * LOG2E), (8, LANES))
        stats[0, t, 0:1] = peak * (SCALE * LOG2E) + jnp.log2(mass)
        stats[0, t, 1:2] = weighted / mass

    loop(0, PARTS, weigh)

    def send_stats(n):
        remote(stats.at[0], stats.at[n], send_sem.at[2], recv_sem.at[3], query_peer(n)[0]).start()

    loop(1, 8, send_stats)
    wait_for(stats.at[pl.ds(1, 7)], recv_sem.at[3])

    def differentiate(t):
        every = [stats[n, t, 0:1] for n in range(8)]
        top = functools.reduce(jnp.maximum, every)
        shares = [jnp.exp2(e - top) for e in every]
        mass = functools.reduce(jnp.add, shares)
        delta = functools.reduce(jnp.add, [s * stats[n, t, 1:2] for n, s in enumerate(shares)]) / mass
        factor = jnp.exp2(peaks[t, 0:1] - top) / mass

        def step(r, carry):
            rows = pl.ds(pl.multiple_of(r * CHUNK, CHUNK), CHUNK)
            probs = scores[t, rows] * factor
            pair[1, t, rows] = probs.astype(jnp.bfloat16)
            pair[0, t, rows] = (probs * (dprobs[t, rows] - delta) * SCALE).astype(jnp.bfloat16)
            return carry

        lax.fori_loop(0, TILE // CHUNK, step, 0)

    loop(0, PARTS, differentiate)

    def key_side(which, r):
        rows = pl.ds(pl.multiple_of(r * LANES, LANES), LANES)
        acc = jnp.zeros((LANES, WIDTH), jnp.float32)
        for t in range(PARTS):
            acc += jnp.dot(
                pair[which, t, rows], qbuf[which, t * LANES : t * LANES + LANES],
                preferred_element_type=jnp.float32,
            )
        return acc, rows

    def give_away(r):
        acc, rows = key_side(1 - c, r)
        give[rows] = acc.astype(jnp.bfloat16)
        remote(give.at[rows], take.at[rows], send_sem.at[3], swap_sem.at[4 + r], sibling).start()

    loop(0, 4, give_away)

    def query_side(t):
        part = lax.dot_general(kbuf[0], pair[0, t], TN, preferred_element_type=jnp.float32)
        part = part.astype(dq_part.dtype)
        dq_part[2 * t] = part[:, :ROWS]
        dq_part[2 * t + 1] = part[:, ROWS:]

    loop(0, PARTS, query_side)

    def send_dq(n):
        where, slot = query_peer(n)
        remote(dq_part.at[slot], dq_took.at[n - 1], send_sem.at[4], recv_sem.at[4], where).start()

    loop(1, 8, send_dq)

    def send_piece(n):
        where, first = owner(n)
        rows = pl.ds(pl.multiple_of(first, 32), 32)
        remote(total.at[rows], gathered.at[n - 1], send_sem.at[5], recv_sem.at[5], where).start()

    def keep(r):
        acc, rows = key_side(c, r)
        wait_for(take.at[rows], swap_sem.at[4 + r])
        total[rows] = (acc + take[rows].astype(jnp.float32)).astype(jnp.bfloat16)
        loop(jnp.where(r == 0, 1, 8 * r), 8 * r + 8, send_piece)

    loop(0, 4, keep)

    wait_for(dq_took, recv_sem.at[4])
    dq = dq_part[own].astype(jnp.float32)
    for n in range(7):
        dq += dq_took[n].astype(jnp.float32)
    dq_out[0] = dq.T.astype(jnp.bfloat16)

    first = pl.ds(pl.multiple_of(yj * 32, 32), 32)
    wait_for(gathered, recv_sem.at[5])
    result = total[first].astype(jnp.float32)
    for n in range(31):
        result += gathered[n].astype(jnp.float32)
    pieces[0] = result.astype(jnp.bfloat16)

    def send_result(n):
        remote(pieces.at[0], pieces.at[n], send_sem.at[6], recv_sem.at[6], head_peer(n)).start()

    loop(1, 8, send_result)
    wait_for(pieces.at[pl.ds(1, 7)], recv_sem.at[6])
    for n in range(YL):
        fl = lax.rem(yl + YL - n, YL)
        rows = pl.ds(pl.multiple_of(lax.rem(fl, 2) * SPAN + lax.div(fl, 2) * 32, 32), 32)
        dk_out[rows] = pieces[2 * n + c]
        dv_out[rows] = pieces[2 * n + 1 - c]

    wait_for(kbuf.at[0, pl.ds(0, 960)], send_sem.at[0])
    wait_for(qbuf.at[:, pl.ds(ROWS, 7 * ROWS)], send_sem.at[1])
    swap_near.wait_send()
    swap_far.wait_send()
    wait_for(stats.at[pl.ds(1, 7)], send_sem.at[2])
    wait_for(give, send_sem.at[3])
    wait_for(dq_took, send_sem.at[4])
    wait_for(gathered, send_sem.at[5])
    wait_for(pieces.at[pl.ds(1, 7)], send_sem.at[6])


def local(queries, keys, values, grad_out, order, segment):
    bf16, f32, i32 = jnp.bfloat16, jnp.float32, jnp.int32
    smem, vmem, hbm = (
        pl.BlockSpec(memory_space=pltpu.SMEM),
        pl.BlockSpec(memory_space=pltpu.VMEM),
        pl.BlockSpec(memory_space=pl.ANY),
    )
    return pl.pallas_call(
        kernel,
        out_shape=(
            jax.ShapeDtypeStruct(queries.shape, bf16),
            jax.ShapeDtypeStruct(keys.shape, bf16),
            jax.ShapeDtypeStruct(values.shape, bf16),
        ),
        in_specs=[smem, vmem, hbm, hbm, hbm, hbm],
        out_specs=(vmem, vmem, vmem),
        scratch_shapes=[
            pltpu.VMEM((2, TILE, WIDTH), bf16),
            pltpu.VMEM((2, ROWS, WIDTH), bf16),
            pltpu.VMEM((2, TILE, WIDTH), bf16),
            pltpu.VMEM((PARTS, TILE, LANES), f32),
            pltpu.VMEM((PARTS, TILE, LANES), f32),
            pltpu.VMEM((2, PARTS, TILE, LANES), bf16),
            pltpu.VMEM((PARTS, 8, LANES), f32),
            pltpu.VMEM((PARTS, 8, LANES), i32),
            pltpu.VMEM((PARTS, 8, LANES), i32),
            pltpu.VMEM((8, PARTS, 2, LANES), f32),
            pltpu.VMEM((TILE, WIDTH), bf16),
            pltpu.VMEM((TILE, WIDTH), bf16),
            pltpu.VMEM((TILE, WIDTH), bf16),
            pltpu.VMEM((31, 32, WIDTH), bf16),
            pltpu.VMEM((8, 32, WIDTH), bf16),
            pltpu.VMEM((8, WIDTH, ROWS), bf16),
            pltpu.VMEM((7, WIDTH, ROWS), bf16),
            pltpu.SemaphoreType.DMA((4,)),
            pltpu.SemaphoreType.DMA((7,)),
            pltpu.SemaphoreType.DMA((7,)),
            pltpu.SemaphoreType.DMA((8,)),
        ],
        compiler_params=pltpu.CompilerParams(
            collective_id=0, has_side_effects=True, vmem_limit_bytes=40 << 20
        ),
        name="attention_backward",
    )(order, segment.reshape(-1, WIDTH), queries, keys, values, grad_out)


def solution(mesh):
    placed = (
        P("head", "ctx", None),
        P("ctx", None),
        P("ctx", None),
        P("head", "ctx", None),
        P(),
        P(),
    )
    return jax.shard_map(
        local,
        mesh=mesh,
        in_specs=placed,
        out_specs=(P("head", "ctx", None), P("ctx", None), P("ctx", None)),
        check_vma=False,
    )
```

```python
import functools
import math

import jax
import jax.numpy as jnp
from jax import lax
from jax.experimental import pallas as pl
from jax.experimental.pallas import tpu as pltpu
from jax.sharding import PartitionSpec as P

YH, Z, X, YL, CORES = 2, 8, 4, 4, 2
DOCS = 6
TOKENS = 8192
SPAN = 64
ROWS = 2 * SPAN
WIDTH = 128
TILE = 1024
LANES = 256
PARTS = TILE // LANES
CHUNK = 128
NEGATIVE = -1e30
FLOOR = -1e20
MESH = pl.DeviceIdType.MESH
SCALE = 1.0 / math.sqrt(WIDTH)
LOG2E = 1.4426950408889634
NT = (((1,), (1,)), ((), ()))
TN = (((0,), (0,)), ((), ()))


def device(yh, z, x, yl, c):
    return {"ctx": yh * (Z * X) + z * X + x, "head": yl * CORES + c}


def kernel(
    order_in, segment_in, q_in, k_in, v_in, go_in, grads,
    places, docs, qbuf, kv, kbuf, scores, dprobs, pair, peaks, lows, highs, stats,
    give, take, kept, total, gathered, pieces, dq_part, dq_took,
    local_sem, send_sem, recv_sem, swap_sem,
):
    i, h = lax.axis_index("ctx"), lax.axis_index("head")
    yh, z, x = lax.div(i, Z * X), lax.rem(lax.div(i, X), Z), lax.rem(i, X)
    yl, c = lax.div(h, CORES), lax.rem(h, CORES)
    yp, yj = lax.rem(yl, 2), lax.div(yl, 2)
    own = yp * X + x
    zs = [lax.rem(z + n, Z) for n in range(Z)]
    xs = [lax.rem(x + n, X) for n in range(X)]
    yls = [lax.rem(yl + n, YL) for n in range(YL)]
    yps, yjs, yhs, cs = (yp, 1 - yp), (yj, 1 - yj), (yh, 1 - yh), (c, 1 - c)
    sibling = device(yh, z, x, yl, 1 - c)

    def query_peer(n):
        tx, tp = xs[n % X], yps[n // X]
        return device(yh, z, tx, yj * 2 + tp, c), tp * X + tx

    def near_peer(n):
        return device(yh, zs[n], x, yl, c)

    def far_peer(n):
        return device(1 - yh, zs[n], x, YL - 1 - yl, c)

    def owner(n):
        g, dz, jj = n // 16, n // 2 % Z, n % 2
        where = device(yhs[g], zs[(Z - dz) % Z], x, yjs[jj] * 2 + yp, c)
        return where, n // 2 * SPAN + yjs[jj] * 32

    def head_peer(n):
        return device(yh, z, x, yls[n // 2], cs[n % 2])

    def remote(src, dst, send, recv, where):
        return pltpu.make_async_remote_copy(
            src_ref=src, dst_ref=dst, send_sem=send, recv_sem=recv,
            device_id=where, device_id_type=MESH,
        )

    def wait_for(ref, sem):
        pltpu.make_async_copy(ref, ref, sem).wait()

    def loop(first, last, body):
        def step(n, carry):
            body(n)
            return carry

        lax.fori_loop(first, last, step, 0)

    def each(first, last, body):
        for n in range(first, last):
            body(n)

    mine = pl.ds(pl.multiple_of(own * ROWS, ROWS), ROWS)
    loads = [
        pltpu.make_async_copy(k_in, kv.at[0], local_sem.at[0]),
        pltpu.make_async_copy(v_in, kv.at[1], local_sem.at[1]),
        pltpu.make_async_copy(q_in.at[0], qbuf.at[0, mine], local_sem.at[2]),
        pltpu.make_async_copy(go_in.at[0], qbuf.at[1, mine], local_sem.at[3]),
        pltpu.make_async_copy(order_in, places, local_sem.at[4]),
        pltpu.make_async_copy(segment_in, docs, local_sem.at[5]),
    ]
    for copy in loads:
        copy.start()

    barrier = pltpu.get_barrier_semaphore()

    def greet(where):
        pl.semaphore_signal(barrier, inc=1, device_id=where, device_id_type=MESH)

    each(1, 32, lambda n: greet(owner(n)[0]))
    each(0, 8, lambda n: greet(far_peer(n)))
    each(1, 8, lambda n: greet(query_peer(n)[0]))
    each(1, 8, lambda n: greet(head_peer(n)))

    for copy in loads:
        copy.wait()
    half = pl.ds(pl.multiple_of(yp * SPAN, SPAN), SPAN)
    other = pl.ds(pl.multiple_of((1 - yp) * SPAN, SPAN), SPAN)
    kbuf[:, :SPAN] = kv[:, half]

    pl.semaphore_wait(barrier, 31 + 8 + 7 + 7)

    def send_far(n):
        rows = pl.ds(512 + n * SPAN, SPAN)
        remote(kv.at[c, other], kbuf.at[c, rows], send_sem.at[0], recv_sem.at[1], far_peer(n)).start()

    def send_near(n):
        rows = pl.ds(n * SPAN, SPAN)
        remote(kv.at[c, half], kbuf.at[c, rows], send_sem.at[0], recv_sem.at[0], near_peer(n)).start()

    def send_query(n):
        remote(qbuf.at[:, mine], qbuf.at[:, mine], send_sem.at[1], recv_sem.at[2], query_peer(n)[0]).start()

    each(0, 8, send_far)
    each(1, 8, send_near)
    each(1, 8, send_query)

    doc = docs[...]
    starts = [
        jnp.sum((doc < d).astype(jnp.int32), axis=(0, 1), keepdims=True) for d in range(1, DOCS)
    ]
    lane = lax.broadcasted_iota(jnp.int32, (8, ROWS), 1)
    for s in range(X):
        ctx = yh * (Z * X) + z * X + s
        first, second = places[2 * ctx], places[2 * ctx + 1]
        place = jnp.where(lane < SPAN, first * SPAN + lane, second * SPAN + lane - SPAN)
        low = jnp.zeros_like(place)
        for start in starts:
            low = jnp.maximum(low, jnp.where(start <= place, start, 0))
        for t in (s, s + X):
            lows[t // 2, :, (t % 2) * ROWS : (t % 2 + 1) * ROWS] = low
            highs[t // 2, :, (t % 2) * ROWS : (t % 2 + 1) * ROWS] = place

    wait_for(kbuf.at[0, pl.ds(SPAN, 448)], recv_sem.at[0])
    near = kbuf.at[c, pl.ds(SPAN, 448)]
    swap_near = remote(near, near, swap_sem.at[0], swap_sem.at[1], sibling)
    swap_near.start()
    wait_for(kbuf.at[0, pl.ds(512, 512)], recv_sem.at[1])
    far = kbuf.at[c, pl.ds(512, 512)]
    swap_far = remote(far, far, swap_sem.at[2], swap_sem.at[3], sibling)
    swap_far.start()
    wait_for(qbuf.at[:, pl.ds(ROWS, 7 * ROWS)], recv_sem.at[2])

    row = lax.broadcasted_iota(jnp.int32, (SPAN, LANES), 0)

    def product(g, t):
        rows = pl.ds(pl.multiple_of(t * LANES, LANES), LANES)
        low, high = lows[t, 0:1, :], highs[t, 0:1, :]
        s = lax.dot_general(
            kbuf[0, g * 512 : g * 512 + 512], qbuf[0, rows], NT, preferred_element_type=jnp.float32
        )
        peak = None if g == 0 else peaks[t]
        for n in range(8):
            ctx = lax.rem(yh + g, 2) * (Z * X) + lax.rem(z + Z - n, Z) * X + x
            place = places[2 * ctx + yp] * SPAN + row
            masked = jnp.where(
                (place >= low) & (place <= high), s[n * SPAN : n * SPAN + SPAN], NEGATIVE
            )
            scores[t, g * 512 + n * SPAN : g * 512 + n * SPAN + SPAN] = masked
            top = jnp.max(masked.reshape(SPAN // 8, 8, LANES), axis=0)
            peak = top if peak is None else jnp.maximum(peak, top)
        peaks[t] = peak
        dprobs[t, g * 512 : g * 512 + 512] = lax.dot_general(
            kbuf[1, g * 512 : g * 512 + 512], qbuf[1, rows], NT, preferred_element_type=jnp.float32
        )

    swap_near.wait_recv()
    loop(0, PARTS, functools.partial(product, 0))
    swap_far.wait_recv()
    loop(0, PARTS, functools.partial(product, 1))

    def summed(a):
        return jnp.sum(a.reshape(CHUNK // 8, 8, LANES), axis=0)

    def weigh(t):
        peak = jnp.maximum(jnp.max(peaks[t], axis=0, keepdims=True), FLOOR)

        def step(r, carry):
            rows = pl.ds(pl.multiple_of(r * CHUNK, CHUNK), CHUNK)
            expo = jnp.exp2((scores[t, rows] - peak) * (SCALE * LOG2E))
            scores[t, rows] = expo
            return carry[0] + summed(expo), carry[1] + summed(expo * dprobs[t, rows])

        zero = jnp.zeros((8, LANES), jnp.float32)
        mass, weighted = lax.fori_loop(0, TILE // CHUNK, step, (zero, zero))
        mass = jnp.maximum(jnp.sum(mass, axis=0, keepdims=True), 1e-30)
        weighted = jnp.sum(weighted, axis=0, keepdims=True)
        peaks[t] = jnp.broadcast_to(peak * (SCALE * LOG2E), (8, LANES))
        stats[0, t, 0:1] = peak * (SCALE * LOG2E) + jnp.log2(mass)
        stats[0, t, 1:2] = weighted / mass

    loop(0, PARTS, weigh)

    def send_stats(n):
        remote(stats.at[0], stats.at[n], send_sem.at[2], recv_sem.at[3], query_peer(n)[0]).start()

    each(1, 8, send_stats)
    wait_for(stats.at[pl.ds(1, 7)], recv_sem.at[3])

    def combine(t):
        every = [stats[n, t, 0:1] for n in range(8)]
        top = functools.reduce(jnp.maximum, every)
        shares = [jnp.exp2(e - top) for e in every]
        mass = functools.reduce(jnp.add, shares)
        delta = functools.reduce(jnp.add, [s * stats[n, t, 1:2] for n, s in enumerate(shares)]) / mass
        factor = jnp.exp2(peaks[t, 0:1] - top) / mass
        peaks[t, 0:1] = factor
        peaks[t, 1:2] = delta

    loop(0, PARTS, combine)

    def differentiate(r):
        def step(n):
            t = lax.div(n, 2)
            rows = pl.ds(pl.multiple_of(r * LANES + lax.rem(n, 2) * CHUNK, CHUNK), CHUNK)
            probs = scores[t, rows] * peaks[t, 0:1]
            pair[1, t, rows] = probs.astype(jnp.bfloat16)
            pair[0, t, rows] = (probs * (dprobs[t, rows] - peaks[t, 1:2]) * SCALE).astype(jnp.bfloat16)

        loop(0, 2 * PARTS, step)

    def key_side(which, rows):
        acc = jnp.zeros((LANES, WIDTH), jnp.float32)
        for t in range(PARTS):
            acc += jnp.dot(
                pair[which, t, rows], qbuf[which, t * LANES : t * LANES + LANES],
                preferred_element_type=jnp.float32,
            )
        return acc

    def send_piece(n):
        where, first = owner(n)
        rows = pl.ds(pl.multiple_of(first, 32), 32)
        remote(total.at[rows], gathered.at[n - 1], send_sem.at[5], recv_sem.at[5], where).start()

    def settle(r):
        rows = pl.ds(r * LANES, LANES)
        wait_for(take.at[rows], swap_sem.at[4 + r])
        total[rows] = (kept[rows] + take[rows].astype(jnp.float32)).astype(jnp.bfloat16)
        each(max(1, 8 * r), 8 * r + 8, send_piece)

    for r in (3, 2, 1, 0):
        rows = pl.ds(r * LANES, LANES)
        differentiate(r)
        give[rows] = key_side(1 - c, rows).astype(jnp.bfloat16)
        remote(give.at[rows], take.at[rows], send_sem.at[3], swap_sem.at[4 + r], sibling).start()
        kept[rows] = key_side(c, rows)
        if r < 3:
            settle(r + 1)
    settle(0)

    def query_side(t):
        part = lax.dot_general(kbuf[0], pair[0, t], TN, preferred_element_type=jnp.float32)
        part = part.astype(dq_part.dtype)
        dq_part[2 * t] = part[:, :ROWS]
        dq_part[2 * t + 1] = part[:, ROWS:]

    loop(0, PARTS, query_side)

    def send_dq(n):
        where, slot = query_peer(n)
        remote(dq_part.at[slot], dq_took.at[n - 1], send_sem.at[4], recv_sem.at[4], where).start()

    each(1, 8, send_dq)

    wait_for(dq_took, recv_sem.at[4])
    dq = dq_part[own].astype(jnp.float32)
    for n in range(7):
        dq += dq_took[n].astype(jnp.float32)
    grads[0] = dq.T.astype(jnp.bfloat16)

    first = pl.ds(pl.multiple_of(yj * 32, 32), 32)
    wait_for(gathered, recv_sem.at[5])
    result = total[first].astype(jnp.float32)
    for n in range(31):
        result += gathered[n].astype(jnp.float32)
    pieces[0] = result.astype(jnp.bfloat16)

    def send_result(n):
        remote(pieces.at[0], pieces.at[n], send_sem.at[6], recv_sem.at[6], head_peer(n)).start()

    each(1, 8, send_result)
    wait_for(pieces.at[pl.ds(1, 7)], recv_sem.at[6])
    for n in range(YL):
        fl = lax.rem(yl + YL - n, YL)
        rows = pl.ds(pl.multiple_of(lax.rem(fl, 2) * SPAN + lax.div(fl, 2) * 32, 32), 32)
        grads[1, rows] = pieces[2 * n + c]
        grads[2, rows] = pieces[2 * n + 1 - c]

    wait_for(kbuf.at[0, pl.ds(0, 960)], send_sem.at[0])
    wait_for(qbuf.at[:, pl.ds(ROWS, 7 * ROWS)], send_sem.at[1])
    swap_near.wait_send()
    swap_far.wait_send()
    wait_for(stats.at[pl.ds(1, 7)], send_sem.at[2])
    wait_for(give, send_sem.at[3])
    wait_for(dq_took, send_sem.at[4])
    wait_for(gathered, send_sem.at[5])
    wait_for(pieces.at[pl.ds(1, 7)], send_sem.at[6])


def local(queries, keys, values, grad_out, order, segment):
    bf16, f32, i32 = jnp.bfloat16, jnp.float32, jnp.int32
    vmem, hbm = pl.BlockSpec(memory_space=pltpu.VMEM), pl.BlockSpec(memory_space=pltpu.HBM)
    grads = pl.pallas_call(
        kernel,
        out_shape=jax.ShapeDtypeStruct((3, ROWS, WIDTH), bf16),
        in_specs=[hbm] * 6,
        out_specs=vmem,
        scratch_shapes=[
            pltpu.SMEM((TOKENS // SPAN,), i32),
            pltpu.VMEM((TOKENS // WIDTH, WIDTH), i32),
            pltpu.VMEM((2, TILE, WIDTH), bf16),
            pltpu.VMEM((2, ROWS, WIDTH), bf16),
            pltpu.VMEM((2, TILE, WIDTH), bf16),
            pltpu.VMEM((PARTS, TILE, LANES), f32),
            pltpu.VMEM((PARTS, TILE, LANES), f32),
            pltpu.VMEM((2, PARTS, TILE, LANES), bf16),
            pltpu.VMEM((PARTS, 8, LANES), f32),
            pltpu.VMEM((PARTS, 8, LANES), i32),
            pltpu.VMEM((PARTS, 8, LANES), i32),
            pltpu.VMEM((8, PARTS, 2, LANES), f32),
            pltpu.VMEM((TILE, WIDTH), bf16),
            pltpu.VMEM((TILE, WIDTH), bf16),
            pltpu.VMEM((TILE, WIDTH), f32),
            pltpu.VMEM((TILE, WIDTH), bf16),
            pltpu.VMEM((31, 32, WIDTH), bf16),
            pltpu.VMEM((8, 32, WIDTH), bf16),
            pltpu.VMEM((8, WIDTH, ROWS), bf16),
            pltpu.VMEM((7, WIDTH, ROWS), bf16),
            pltpu.SemaphoreType.DMA((6,)),
            pltpu.SemaphoreType.DMA((7,)),
            pltpu.SemaphoreType.DMA((7,)),
            pltpu.SemaphoreType.DMA((8,)),
        ],
        compiler_params=pltpu.CompilerParams(
            collective_id=0, has_side_effects=True, vmem_limit_bytes=63 << 20
        ),
        name="attention_backward",
    )(order, segment.reshape(-1, WIDTH), queries, keys, values, grad_out)
    return grads[0:1], grads[1], grads[2]


def solution(mesh):
    placed = (
        P("head", "ctx", None),
        P("ctx", None),
        P("ctx", None),
        P("head", "ctx", None),
        P(),
        P(),
    )
    return jax.shard_map(
        local,
        mesh=mesh,
        in_specs=placed,
        out_specs=(P("head", "ctx", None), P("ctx", None), P("ctx", None)),
        check_vma=False,
    )
```

```python
import functools
import math

import jax
import jax.numpy as jnp
from jax import lax
from jax.experimental import pallas as pl
from jax.experimental.pallas import tpu as pltpu
from jax.sharding import PartitionSpec as P

YH, Z, X, YL, CORES = 2, 8, 4, 4, 2
DOCS = 6
TOKENS = 8192
SPAN = 64
ROWS = 2 * SPAN
WIDTH = 128
TILE = 1024
LANES = 256
PARTS = TILE // LANES
CHUNK = 128
NEGATIVE = -1e30
FLOOR = -1e20
MESH = pl.DeviceIdType.MESH
SCALE = 1.0 / math.sqrt(WIDTH)
LOG2E = 1.4426950408889634
NT = (((1,), (1,)), ((), ()))
TN = (((0,), (0,)), ((), ()))


def device(yh, z, x, yl, c):
    return {"ctx": yh * (Z * X) + z * X + x, "head": yl * CORES + c}


def kernel(
    order_in, segment_in, q_in, k_in, v_in, go_in, grads,
    places, docs, qbuf, kv, kbuf, scores, dprobs, pair, peaks, masses, weights, lows, highs,
    logs, deltas, give, take, kept, total, gathered, pieces, dq_part, dq_took,
    local_sem, send_sem, recv_sem, swap_sem, take_sem,
):
    i, h = lax.axis_index("ctx"), lax.axis_index("head")
    yh, z, x = lax.div(i, Z * X), lax.rem(lax.div(i, X), Z), lax.rem(i, X)
    yl, c = lax.div(h, CORES), lax.rem(h, CORES)
    yp, yj = lax.rem(yl, 2), lax.div(yl, 2)
    own = yp * X + x
    zs = [lax.rem(z + n, Z) for n in range(Z)]
    xs = [lax.rem(x + n, X) for n in range(X)]
    yls = [lax.rem(yl + n, YL) for n in range(YL)]
    yps, yjs, yhs, cs = (yp, 1 - yp), (yj, 1 - yj), (yh, 1 - yh), (c, 1 - c)
    sibling = device(yh, z, x, yl, 1 - c)

    def query_peer(n):
        tx, tp = xs[n % X], yps[n // X]
        return device(yh, z, tx, yj * 2 + tp, c), tp * X + tx

    def near_peer(n):
        return device(yh, zs[n], x, yl, c)

    def far_peer(n):
        return device(1 - yh, zs[n], x, YL - 1 - yl, c)

    def owner(n):
        g, dz, jj = n // 16, n // 2 % 4 * 2 + n // 8 % 2, n % 2
        where = device(yhs[g], zs[(Z - dz) % Z], x, yjs[jj] * 2 + yp, c)
        return where, n // 2 * SPAN + yjs[jj] * 32

    def head_peer(n):
        return device(yh, z, x, yls[n // 2], cs[n % 2])

    def remote(src, dst, send, recv, where):
        return pltpu.make_async_remote_copy(
            src_ref=src, dst_ref=dst, send_sem=send, recv_sem=recv,
            device_id=where, device_id_type=MESH,
        )

    def wait_for(ref, sem):
        pltpu.make_async_copy(ref, ref, sem).wait()

    def loop(first, last, body):
        def step(n, carry):
            body(n)
            return carry

        lax.fori_loop(first, last, step, 0)

    def each(first, last, body):
        for n in range(first, last):
            body(n)

    mine = pl.ds(pl.multiple_of(own * ROWS, ROWS), ROWS)
    loads = [
        pltpu.make_async_copy(k_in, kv.at[0], local_sem.at[0]),
        pltpu.make_async_copy(v_in, kv.at[1], local_sem.at[1]),
        pltpu.make_async_copy(q_in.at[0], qbuf.at[0, mine], local_sem.at[2]),
        pltpu.make_async_copy(go_in.at[0], qbuf.at[1, mine], local_sem.at[3]),
        pltpu.make_async_copy(order_in, places, local_sem.at[4]),
        pltpu.make_async_copy(segment_in, docs, local_sem.at[5]),
    ]
    for copy in loads:
        copy.start()

    barrier = pltpu.get_barrier_semaphore()

    def greet(where):
        pl.semaphore_signal(barrier, inc=1, device_id=where, device_id_type=MESH)

    each(1, 32, lambda n: greet(owner(n)[0]))
    each(0, 8, lambda n: greet(far_peer(n)))
    each(1, 8, lambda n: greet(query_peer(n)[0]))
    each(1, 8, lambda n: greet(head_peer(n)))

    for copy in loads:
        copy.wait()
    half = pl.ds(pl.multiple_of(yp * SPAN, SPAN), SPAN)
    other = pl.ds(pl.multiple_of((1 - yp) * SPAN, SPAN), SPAN)

    pl.semaphore_wait(barrier, 31 + 8 + 7 + 7)

    def send_far(a, m):
        rows = pl.ds(pl.multiple_of(512 + c * 256 + m * SPAN, SPAN), SPAN)
        where = device(1 - yh, lax.rem(z + 2 * m + c, Z), x, YL - 1 - yl, c)
        remote(kv.at[a, other], kbuf.at[a, rows], send_sem.at[0], recv_sem.at[2 * a + 1], where).start()

    def send_near(a, m):
        rows = pl.ds(pl.multiple_of(c * 256 + m * SPAN, SPAN), SPAN)
        where = device(yh, lax.rem(z + 2 * m + c, Z), x, yl, c)

        def send():
            remote(kv.at[a, half], kbuf.at[a, rows], send_sem.at[0], recv_sem.at[2 * a], where).start()

        if m > 0:
            send()
            return
        pl.when(c == 1)(send)

        @pl.when(c == 0)
        def _():
            pltpu.make_async_copy(kv.at[a, half], kbuf.at[a, pl.ds(0, SPAN)], recv_sem.at[2 * a]).start()

    def send_query(a, n):
        remote(
            qbuf.at[a, mine], qbuf.at[a, mine], send_sem.at[1], recv_sem.at[4 + a], query_peer(n)[0]
        ).start()

    for a in range(2):
        for m in range(4):
            send_far(a, m)
        for m in range(4):
            send_near(a, m)
        for n in range(1, 8):
            send_query(a, n)

    doc = docs[...]
    starts = [
        jnp.sum((doc < d).astype(jnp.int32), axis=(0, 1), keepdims=True) for d in range(1, DOCS)
    ]
    lane = lax.broadcasted_iota(jnp.int32, (8, ROWS), 1)
    for s in range(X):
        ctx = yh * (Z * X) + z * X + s
        first, second = places[2 * ctx], places[2 * ctx + 1]
        place = jnp.where(lane < SPAN, first * SPAN + lane, second * SPAN + lane - SPAN)
        low = jnp.zeros_like(place)
        for start in starts:
            low = jnp.maximum(low, jnp.where(start <= place, start, 0))
        for t in (s, s + X):
            lows[t // 2, :, (t % 2) * ROWS : (t % 2 + 1) * ROWS] = low
            highs[t // 2, :, (t % 2) * ROWS : (t % 2 + 1) * ROWS] = place

    def hand_over(a, g):
        rows = pl.ds(pl.multiple_of(g * 512 + c * 256, 256), 256)
        wait_for(kbuf.at[a, rows], recv_sem.at[2 * a + g])
        remote(kbuf.at[a, rows], kbuf.at[a, rows], swap_sem.at[4], swap_sem.at[2 * a + g], sibling).start()

    def handed(a, g):
        rows = pl.ds(pl.multiple_of(g * 512 + (1 - c) * 256, 256), 256)
        wait_for(kbuf.at[a, rows], swap_sem.at[2 * a + g])

    hand_over(0, 0)
    hand_over(0, 1)
    wait_for(qbuf.at[0, pl.ds(ROWS, 7 * ROWS)], recv_sem.at[4])

    row = lax.broadcasted_iota(jnp.int32, (SPAN, LANES), 0)

    def product(g, t):
        rows = pl.ds(pl.multiple_of(t * LANES, LANES), LANES)
        low, high = lows[t, 0:1, :], highs[t, 0:1, :]
        s = lax.dot_general(
            kbuf[0, g * 512 : g * 512 + 512], qbuf[0, rows], NT, preferred_element_type=jnp.float32
        )
        peak = None if g == 0 else peaks[t]
        for n in range(8):
            behind = zs[(Z - (n % 4 * 2 + n // 4)) % Z]
            ctx = yhs[g] * (Z * X) + behind * X + x
            place = places[2 * ctx + yp] * SPAN + row
            masked = jnp.where(
                (place >= low) & (place <= high), s[n * SPAN : n * SPAN + SPAN], NEGATIVE
            )
            scores[t, g * 512 + n * SPAN : g * 512 + n * SPAN + SPAN] = masked
            top = jnp.max(masked.reshape(SPAN // 8, 8, LANES), axis=0)
            peak = top if peak is None else jnp.maximum(peak, top)
        peaks[t] = peak

    handed(0, 0)
    loop(0, PARTS, functools.partial(product, 0))
    handed(0, 1)
    loop(0, PARTS, functools.partial(product, 1))
    hand_over(1, 0)
    hand_over(1, 1)

    def weigh(t):
        peak = jnp.maximum(jnp.max(peaks[t], axis=0, keepdims=True), FLOOR)

        def step(r, carry):
            rows = pl.ds(pl.multiple_of(r * CHUNK, CHUNK), CHUNK)
            expo = jnp.exp2((scores[t, rows] - peak) * (SCALE * LOG2E))
            scores[t, rows] = expo
            return carry + jnp.sum(expo.reshape(CHUNK // 8, 8, LANES), axis=0)

        mass = lax.fori_loop(0, TILE // CHUNK, step, jnp.zeros((8, LANES), jnp.float32))
        mass = jnp.maximum(jnp.sum(mass, axis=0, keepdims=True), 1e-30)
        peak = peak * (SCALE * LOG2E)
        peaks[t, 0:1] = peak
        masses[t] = mass
        logs[0, t] = peak + jnp.log2(mass)

    loop(0, PARTS, weigh)

    def send_logs(n):
        remote(logs.at[0], logs.at[n], send_sem.at[2], recv_sem.at[6], query_peer(n)[0]).start()

    each(1, 8, send_logs)

    def cotangent(g, t):
        rows = pl.ds(pl.multiple_of(t * LANES, LANES), LANES)
        d = lax.dot_general(
            kbuf[1, g * 512 : g * 512 + 512], qbuf[1, rows], NT, preferred_element_type=jnp.float32
        )
        dprobs[t, g * 512 : g * 512 + 512] = d
        weighted = jnp.sum((scores[t, g * 512 : g * 512 + 512] * d).reshape(64, 8, LANES), axis=0)
        if g == 0:
            weights[t] = weighted
        else:
            weighted = jnp.sum(weights[t] + weighted, axis=0, keepdims=True)
            deltas[0, t] = weighted / masses[t]

    wait_for(qbuf.at[1, pl.ds(ROWS, 7 * ROWS)], recv_sem.at[5])
    handed(1, 0)
    loop(0, PARTS, functools.partial(cotangent, 0))
    handed(1, 1)
    loop(0, PARTS, functools.partial(cotangent, 1))

    def send_deltas(n):
        remote(deltas.at[0], deltas.at[n], send_sem.at[7], recv_sem.at[7], query_peer(n)[0]).start()

    each(1, 8, send_deltas)

    def lse_of(t):
        every = [logs[n, t] for n in range(8)]
        top = functools.reduce(jnp.maximum, every)
        shares = [jnp.exp2(e - top) for e in every]
        return top, shares, functools.reduce(jnp.add, shares)

    def normalize(t):
        top, _, mass = lse_of(t)
        peaks[t, 0:1] = jnp.exp2(peaks[t, 0:1] - top) / mass

    def center(t):
        _, shares, mass = lse_of(t)
        peaks[t, 1:2] = functools.reduce(jnp.add, [s * deltas[n, t] for n, s in enumerate(shares)]) / mass

    def place_of(r, n):
        return lax.div(n, 2), pl.ds(pl.multiple_of(r * LANES + lax.rem(n, 2) * CHUNK, CHUNK), CHUNK)

    def value_weights(r):
        def step(n):
            t, rows = place_of(r, n)
            pair[1, t, rows] = (scores[t, rows] * peaks[t, 0:1]).astype(jnp.bfloat16)

        loop(0, 2 * PARTS, step)

    def key_weights(r):
        def step(n):
            t, rows = place_of(r, n)
            probs = scores[t, rows] * peaks[t, 0:1]
            pair[0, t, rows] = (probs * (dprobs[t, rows] - peaks[t, 1:2]) * SCALE).astype(jnp.bfloat16)

        loop(0, 2 * PARTS, step)

    def key_side(which, rows):
        acc = jnp.zeros((LANES, WIDTH), jnp.float32)
        for t in range(PARTS):
            acc += jnp.dot(
                pair[which, t, rows], qbuf[which, t * LANES : t * LANES + LANES],
                preferred_element_type=jnp.float32,
            )
        return acc

    def send_piece(n):
        where, first = owner(n)
        rows = pl.ds(pl.multiple_of(first, 32), 32)
        remote(total.at[rows], gathered.at[n - 1], send_sem.at[5], recv_sem.at[9], where).start()

    def settle(r):
        rows = pl.ds(r * LANES, LANES)
        wait_for(take.at[rows], take_sem.at[r])
        total[rows] = (kept[rows] + take[rows].astype(jnp.float32)).astype(jnp.bfloat16)
        each(max(1, 8 * r), 8 * r + 8, send_piece)

    def one_side(which, weigh_chunk):
        keeps = c == which
        for r in (3, 2, 1, 0):
            rows = pl.ds(r * LANES, LANES)
            weigh_chunk(r)
            acc = key_side(which, rows)

            @pl.when(jnp.logical_not(keeps))
            def _():
                give[rows] = acc.astype(jnp.bfloat16)
                remote(give.at[rows], take.at[rows], send_sem.at[3], take_sem.at[r], sibling).start()

            @pl.when(keeps)
            def _():
                kept[rows] = acc
                if r < 3:
                    settle(r + 1)
        pl.when(keeps)(lambda: settle(0))

    wait_for(logs.at[pl.ds(1, 7)], recv_sem.at[6])
    loop(0, PARTS, normalize)
    one_side(1, value_weights)
    wait_for(deltas.at[pl.ds(1, 7)], recv_sem.at[7])
    loop(0, PARTS, center)
    one_side(0, key_weights)

    def query_side(t):
        part = lax.dot_general(kbuf[0], pair[0, t], TN, preferred_element_type=jnp.float32)
        part = part.astype(dq_part.dtype)
        dq_part[2 * t] = part[:, :ROWS]
        dq_part[2 * t + 1] = part[:, ROWS:]

    loop(0, PARTS, query_side)

    def send_dq(n):
        where, slot = query_peer(n)
        remote(dq_part.at[slot], dq_took.at[n - 1], send_sem.at[4], recv_sem.at[8], where).start()

    each(1, 8, send_dq)

    wait_for(dq_took, recv_sem.at[8])
    dq = dq_part[own].astype(jnp.float32)
    for n in range(7):
        dq += dq_took[n].astype(jnp.float32)
    grads[0] = dq.T.astype(jnp.bfloat16)

    first = pl.ds(pl.multiple_of(yj * 32, 32), 32)
    wait_for(gathered, recv_sem.at[9])
    result = total[first].astype(jnp.float32)
    for n in range(31):
        result += gathered[n].astype(jnp.float32)
    pieces[0] = result.astype(jnp.bfloat16)

    def send_result(n):
        remote(pieces.at[0], pieces.at[n], send_sem.at[6], recv_sem.at[10], head_peer(n)).start()

    each(1, 8, send_result)
    wait_for(pieces.at[pl.ds(1, 7)], recv_sem.at[10])
    for n in range(YL):
        fl = lax.rem(yl + YL - n, YL)
        rows = pl.ds(pl.multiple_of(lax.rem(fl, 2) * SPAN + lax.div(fl, 2) * 32, 32), 32)
        grads[1, rows] = pieces[2 * n + c]
        grads[2, rows] = pieces[2 * n + 1 - c]

    pl.when(c == 0)(lambda: wait_for(kbuf.at[0, pl.ds(0, 896)], send_sem.at[0]))
    pl.when(c == 1)(lambda: wait_for(kbuf.at[0], send_sem.at[0]))
    wait_for(qbuf.at[:, pl.ds(ROWS, 7 * ROWS)], send_sem.at[1])
    wait_for(kbuf.at[0], swap_sem.at[4])
    wait_for(logs.at[pl.ds(1, 7)], send_sem.at[2])
    wait_for(deltas.at[pl.ds(1, 7)], send_sem.at[7])
    wait_for(give, send_sem.at[3])
    wait_for(dq_took, send_sem.at[4])
    wait_for(gathered, send_sem.at[5])
    wait_for(pieces.at[pl.ds(1, 7)], send_sem.at[6])


def local(queries, keys, values, grad_out, order, segment):
    bf16, f32, i32 = jnp.bfloat16, jnp.float32, jnp.int32
    vmem, hbm = pl.BlockSpec(memory_space=pltpu.VMEM), pl.BlockSpec(memory_space=pltpu.HBM)
    grads = pl.pallas_call(
        kernel,
        out_shape=pltpu.VMEM((3, ROWS, WIDTH), bf16),
        in_specs=[hbm] * 6,
        out_specs=vmem,
        scratch_shapes=[
            pltpu.SMEM((TOKENS // SPAN,), i32),
            pltpu.VMEM((TOKENS // WIDTH, WIDTH), i32),
            pltpu.VMEM((2, TILE, WIDTH), bf16),
            pltpu.VMEM((2, ROWS, WIDTH), bf16),
            pltpu.VMEM((2, TILE, WIDTH), bf16),
            pltpu.VMEM((PARTS, TILE, LANES), f32),
            pltpu.VMEM((PARTS, TILE, LANES), f32),
            pltpu.VMEM((2, PARTS, TILE, LANES), bf16),
            pltpu.VMEM((PARTS, 8, LANES), f32),
            pltpu.VMEM((PARTS, 1, LANES), f32),
            pltpu.VMEM((PARTS, 8, LANES), f32),
            pltpu.VMEM((PARTS, 8, LANES), i32),
            pltpu.VMEM((PARTS, 8, LANES), i32),
            pltpu.VMEM((8, PARTS, 1, LANES), f32),
            pltpu.VMEM((8, PARTS, 1, LANES), f32),
            pltpu.VMEM((TILE, WIDTH), bf16),
            pltpu.VMEM((TILE, WIDTH), bf16),
            pltpu.VMEM((TILE, WIDTH), f32),
            pltpu.VMEM((TILE, WIDTH), bf16),
            pltpu.VMEM((31, 32, WIDTH), bf16),
            pltpu.VMEM((8, 32, WIDTH), bf16),
            pltpu.VMEM((8, WIDTH, ROWS), bf16),
            pltpu.VMEM((7, WIDTH, ROWS), bf16),
            pltpu.SemaphoreType.DMA((6,)),
            pltpu.SemaphoreType.DMA((8,)),
            pltpu.SemaphoreType.DMA((11,)),
            pltpu.SemaphoreType.DMA((5,)),
            pltpu.SemaphoreType.DMA((4,)),
        ],
        compiler_params=pltpu.CompilerParams(
            collective_id=0, has_side_effects=True, vmem_limit_bytes=55 << 20
        ),
        name="attention_backward",
    )(order, segment.reshape(-1, WIDTH), queries, keys, values, grad_out)
    return grads[0:1], grads[1], grads[2]


def solution(mesh):
    placed = (
        P("head", "ctx", None),
        P("ctx", None),
        P("ctx", None),
        P("head", "ctx", None),
        P(),
        P(),
    )
    return jax.shard_map(
        local,
        mesh=mesh,
        in_specs=placed,
        out_specs=(P("head", "ctx", None), P("ctx", None), P("ctx", None)),
        check_vma=False,
    )
```

```python
import functools
import math

import jax
import jax.numpy as jnp
from jax import lax
from jax.experimental import pallas as pl
from jax.experimental.pallas import tpu as pltpu
from jax.sharding import PartitionSpec as P

YH, Z, X, YL, CORES = 2, 8, 4, 4, 2
DOCS = 6
TOKENS = 8192
SPAN = 64
HALF = SPAN // 2
ROWS = 2 * SPAN
WIDTH = 128
TILE = 1024
LANES = 256
PARTS = TILE // LANES
CHUNK = 128
NEGATIVE = -1e30
FLOOR = -1e20
MESH = pl.DeviceIdType.MESH
SCALE = 1.0 / math.sqrt(WIDTH)
LOG2E = 1.4426950408889634
NT = (((1,), (1,)), ((), ()))
TN = (((0,), (0,)), ((), ()))


def device(yh, z, x, yl, c):
    return {"ctx": yh * (Z * X) + z * X + x, "head": yl * CORES + c}


def kernel(
    order_in, segment_in, q_in, k_in, v_in, go_in, grads,
    places, docs, qbuf, kv, kbuf, scores, dprobs, pair, peaks, masses, weights, lows, highs,
    logs, deltas, give, take, total, gathered, pieces, dq_part, dq_took,
    local_sem, send_sem, recv_sem, swap_sem, take_sem,
):
    i, h = lax.axis_index("ctx"), lax.axis_index("head")
    yh, z, x = lax.div(i, Z * X), lax.rem(lax.div(i, X), Z), lax.rem(i, X)
    yl, c = lax.div(h, CORES), lax.rem(h, CORES)
    yp, yj = lax.rem(yl, 2), lax.div(yl, 2)
    own = yp * X + x
    zs = [lax.rem(z + n, Z) for n in range(Z)]
    xs = [lax.rem(x + n, X) for n in range(X)]
    yls = [lax.rem(yl + n, YL) for n in range(YL)]
    yps, yjs, yhs, cs = (yp, 1 - yp), (yj, 1 - yj), (yh, 1 - yh), (c, 1 - c)
    sibling = device(yh, z, x, yl, 1 - c)

    def query_peer(n):
        tx, tp = xs[n % X], yps[n // X]
        return device(yh, z, tx, yj * 2 + tp, c), tp * X + tx

    def near_peer(n):
        return device(yh, zs[n], x, yl, c)

    def far_peer(n):
        return device(1 - yh, zs[n], x, YL - 1 - yl, c)

    def owner(n):
        g, dz, jj = n // 16, n // 2 % 4 * 2 + n // 8 % 2, n % 2
        where = device(yhs[g], zs[(Z - dz) % Z], x, yjs[jj] * 2 + yp, c)
        return where, n // 2 * HALF + yjs[jj] * 16

    def head_peer(n):
        return device(yh, z, x, yls[n // 2], cs[n % 2])

    def remote(src, dst, send, recv, where):
        return pltpu.make_async_remote_copy(
            src_ref=src, dst_ref=dst, send_sem=send, recv_sem=recv,
            device_id=where, device_id_type=MESH,
        )

    def wait_for(ref, sem):
        pltpu.make_async_copy(ref, ref, sem).wait()

    def loop(first, last, body):
        def step(n, carry):
            body(n)
            return carry

        lax.fori_loop(first, last, step, 0)

    def each(first, last, body):
        for n in range(first, last):
            body(n)

    mine = pl.ds(pl.multiple_of(own * ROWS, ROWS), ROWS)
    loads = [
        pltpu.make_async_copy(k_in, kv.at[0], local_sem.at[0]),
        pltpu.make_async_copy(v_in, kv.at[1], local_sem.at[1]),
        pltpu.make_async_copy(q_in.at[0], qbuf.at[0, mine], local_sem.at[2]),
        pltpu.make_async_copy(go_in.at[0], qbuf.at[1, mine], local_sem.at[3]),
        pltpu.make_async_copy(order_in, places, local_sem.at[4]),
        pltpu.make_async_copy(segment_in, docs, local_sem.at[5]),
    ]
    for copy in loads:
        copy.start()

    barrier = pltpu.get_barrier_semaphore()

    def greet(where):
        pl.semaphore_signal(barrier, inc=1, device_id=where, device_id_type=MESH)

    each(1, 32, lambda n: greet(owner(n)[0]))
    each(0, 8, lambda n: greet(far_peer(n)))
    each(1, 8, lambda n: greet(query_peer(n)[0]))
    each(1, 8, lambda n: greet(head_peer(n)))

    for copy in loads:
        copy.wait()
    pl.semaphore_wait(barrier, 31 + 8 + 7 + 7)

    def send_far(a, m):
        rows = pl.ds(pl.multiple_of(256 + c * 128 + m * HALF, HALF), HALF)
        where = device(1 - yh, lax.rem(z + 2 * m + c, Z), x, YL - 1 - yl, c)
        remote(kv.at[a, 1 - yp], kbuf.at[a, :, rows], send_sem.at[0], recv_sem.at[2 * a + 1], where).start()

    def send_near(a, m):
        rows = pl.ds(pl.multiple_of(c * 128 + m * HALF, HALF), HALF)
        where = device(yh, lax.rem(z + 2 * m + c, Z), x, yl, c)

        def send():
            remote(kv.at[a, yp], kbuf.at[a, :, rows], send_sem.at[0], recv_sem.at[2 * a], where).start()

        if m > 0:
            send()
            return
        pl.when(c == 1)(send)

        @pl.when(c == 0)
        def _():
            pltpu.make_async_copy(kv.at[a, yp], kbuf.at[a, :, pl.ds(0, HALF)], recv_sem.at[2 * a]).start()

    def send_query(a, n):
        remote(
            qbuf.at[a, mine], qbuf.at[a, mine], send_sem.at[1], recv_sem.at[4 + a], query_peer(n)[0]
        ).start()

    for a in range(2):
        for m in range(4):
            send_far(a, m)
        for m in range(4):
            send_near(a, m)
        for n in range(1, 8):
            send_query(a, n)

    doc = docs[...]
    starts = [
        jnp.sum((doc < d).astype(jnp.int32), axis=(0, 1), keepdims=True) for d in range(1, DOCS)
    ]
    lane = lax.broadcasted_iota(jnp.int32, (8, ROWS), 1)
    for s in range(X):
        ctx = yh * (Z * X) + z * X + s
        first, second = places[2 * ctx], places[2 * ctx + 1]
        place = jnp.where(lane < SPAN, first * SPAN + lane, second * SPAN + lane - SPAN)
        low = jnp.zeros_like(place)
        for start in starts:
            low = jnp.maximum(low, jnp.where(start <= place, start, 0))
        for t in (s, s + X):
            lows[t // 2, :, (t % 2) * ROWS : (t % 2 + 1) * ROWS] = low
            highs[t // 2, :, (t % 2) * ROWS : (t % 2 + 1) * ROWS] = place

    def hand_over(a, g):
        rows = pl.ds(pl.multiple_of(g * 256 + c * 128, 128), 128)
        block = kbuf.at[a, :, rows]
        wait_for(block, recv_sem.at[2 * a + g])
        remote(block, block, swap_sem.at[4], swap_sem.at[2 * a + g], sibling).start()

    def handed(a, g):
        rows = pl.ds(pl.multiple_of(g * 256 + (1 - c) * 128, 128), 128)
        wait_for(kbuf.at[a, :, rows], swap_sem.at[2 * a + g])

    hand_over(0, 0)
    hand_over(0, 1)
    wait_for(qbuf.at[0, pl.ds(ROWS, 7 * ROWS)], recv_sem.at[4])

    row = lax.broadcasted_iota(jnp.int32, (HALF, LANES), 0)

    def product(g, t):
        rows = pl.ds(pl.multiple_of(t * LANES, LANES), LANES)
        low, high = lows[t, 0:1, :], highs[t, 0:1, :]
        peak = None if g == 0 else peaks[t]
        for b in range(2):
            s = lax.dot_general(
                kbuf[0, b, g * 256 : g * 256 + 256], qbuf[0, rows], NT, preferred_element_type=jnp.float32
            )
            for n in range(8):
                behind = zs[(Z - (n % 4 * 2 + n // 4)) % Z]
                ctx = yhs[g] * (Z * X) + behind * X + x
                place = places[2 * ctx + yp] * SPAN + b * HALF + row
                masked = jnp.where(
                    (place >= low) & (place <= high), s[n * HALF : n * HALF + HALF], NEGATIVE
                )
                first = b * 512 + g * 256 + n * HALF
                scores[t, first : first + HALF] = masked
                top = jnp.max(masked.reshape(HALF // 8, 8, LANES), axis=0)
                peak = top if peak is None else jnp.maximum(peak, top)
        peaks[t] = peak

    handed(0, 0)
    loop(0, PARTS, functools.partial(product, 0))
    handed(0, 1)
    loop(0, PARTS, functools.partial(product, 1))
    def weigh(t):
        peak = jnp.maximum(jnp.max(peaks[t], axis=0, keepdims=True), FLOOR)

        def step(r, carry):
            rows = pl.ds(pl.multiple_of(r * CHUNK, CHUNK), CHUNK)
            expo = jnp.exp2((scores[t, rows] - peak) * (SCALE * LOG2E))
            scores[t, rows] = expo
            return carry + jnp.sum(expo.reshape(CHUNK // 8, 8, LANES), axis=0)

        mass = lax.fori_loop(0, TILE // CHUNK, step, jnp.zeros((8, LANES), jnp.float32))
        mass = jnp.maximum(jnp.sum(mass, axis=0, keepdims=True), 1e-30)
        peak = peak * (SCALE * LOG2E)
        peaks[t, 0:1] = peak
        masses[t] = mass
        logs[0, t] = peak + jnp.log2(mass)

    loop(0, PARTS, weigh)

    def send_logs(n):
        remote(logs.at[0], logs.at[n], send_sem.at[2], recv_sem.at[6], query_peer(n)[0]).start()

    each(1, 8, send_logs)
    hand_over(1, 0)
    hand_over(1, 1)

    def cotangent(g, t):
        rows = pl.ds(pl.multiple_of(t * LANES, LANES), LANES)
        weighted = jnp.zeros((8, LANES), jnp.float32)
        for b in range(2):
            keys = slice(b * 512 + g * 256, b * 512 + g * 256 + 256)
            d = lax.dot_general(
                kbuf[1, b, g * 256 : g * 256 + 256], qbuf[1, rows], NT, preferred_element_type=jnp.float32
            )
            dprobs[t, keys] = d
            weighted += jnp.sum((scores[t, keys] * d).reshape(32, 8, LANES), axis=0)
        if g == 0:
            weights[t] = weighted
        else:
            weighted = jnp.sum(weights[t] + weighted, axis=0, keepdims=True)
            deltas[0, t] = weighted / masses[t]

    wait_for(qbuf.at[1, pl.ds(ROWS, 7 * ROWS)], recv_sem.at[5])
    handed(1, 0)
    loop(0, PARTS, functools.partial(cotangent, 0))
    handed(1, 1)
    loop(0, PARTS, functools.partial(cotangent, 1))

    def send_deltas(n):
        remote(deltas.at[0], deltas.at[n], send_sem.at[7], recv_sem.at[7], query_peer(n)[0]).start()

    each(1, 8, send_deltas)

    def lse_of(t):
        every = [logs[n, t] for n in range(8)]
        top = functools.reduce(jnp.maximum, every)
        shares = [jnp.exp2(e - top) for e in every]
        return top, shares, functools.reduce(jnp.add, shares)

    def normalize(t):
        top, _, mass = lse_of(t)
        peaks[t, 0:1] = jnp.exp2(peaks[t, 0:1] - top) / mass

    def center(t):
        _, shares, mass = lse_of(t)
        peaks[t, 1:2] = functools.reduce(jnp.add, [s * deltas[n, t] for n, s in enumerate(shares)]) / mass

    def value_weights(first):
        def step(n):
            t, rows = lax.div(n, 2), pl.ds(pl.multiple_of(first + lax.rem(n, 2) * CHUNK, CHUNK), CHUNK)
            pair[1, t, rows] = (scores[t, rows] * peaks[t, 0:1]).astype(jnp.bfloat16)

        loop(0, 2 * PARTS, step)

    def key_weights(first):
        def step(n):
            t, rows = lax.div(n, 2), pl.ds(pl.multiple_of(first + lax.rem(n, 2) * CHUNK, CHUNK), CHUNK)
            probs = scores[t, rows] * peaks[t, 0:1]
            pair[0, t, rows] = (probs * (dprobs[t, rows] - peaks[t, 1:2]) * SCALE).astype(jnp.bfloat16)

        loop(0, 2 * PARTS, step)

    def key_side(which, first):
        acc = jnp.zeros((LANES, WIDTH), jnp.float32)
        for t in range(PARTS):
            acc += jnp.dot(
                pair[which, t, pl.ds(first, LANES)], qbuf[which, t * LANES : t * LANES + LANES],
                preferred_element_type=jnp.float32,
            )
        return acc

    def send_piece(which, n):
        where, first = owner(n)
        rows = pl.ds(pl.multiple_of(first, 16), 16)
        remote(
            total.at[which, rows], gathered.at[which, n - 1],
            send_sem.at[5], recv_sem.at[9 + which], where,
        ).start()

    def one_side(which, weigh_chunk):
        for r in (1, 0):
            first = pl.multiple_of((1 - c) * 512 + r * LANES, LANES)
            rows = pl.ds(r * LANES, LANES)
            weigh_chunk(first)
            give[which, rows] = key_side(which, first).astype(jnp.bfloat16)
            remote(
                give.at[which, rows], take.at[which, rows],
                send_sem.at[3], take_sem.at[2 * which + r], sibling,
            ).start()
        for r in (1, 0):
            first = pl.multiple_of(c * 512 + r * LANES, LANES)
            rows = pl.ds(r * LANES, LANES)
            weigh_chunk(first)
            acc = key_side(which, first)
            wait_for(take.at[which, rows], take_sem.at[2 * which + r])
            total[which, rows] = (acc + take[which, rows].astype(jnp.float32)).astype(jnp.bfloat16)
            each(max(1, 16 * r), 16 * r + 16, functools.partial(send_piece, which))

    def conclude(which):
        wait_for(gathered.at[which], recv_sem.at[9 + which])
        result = total[which, pl.ds(pl.multiple_of(yj * 16, 16), 16)].astype(jnp.float32)
        for n in range(31):
            result += gathered[which, n].astype(jnp.float32)
        pieces[which, 0] = result.astype(jnp.bfloat16)
        for n in range(1, 8):
            remote(
                pieces.at[which, 0], pieces.at[which, n],
                send_sem.at[6], recv_sem.at[11 + which], head_peer(n),
            ).start()

    wait_for(logs.at[pl.ds(1, 7)], recv_sem.at[6])
    loop(0, PARTS, normalize)
    one_side(1, value_weights)
    wait_for(deltas.at[pl.ds(1, 7)], recv_sem.at[7])
    loop(0, PARTS, center)
    one_side(0, key_weights)

    def query_side(t):
        keys = kbuf[0].reshape(TILE, WIDTH)
        part = lax.dot_general(keys, pair[0, t], TN, preferred_element_type=jnp.float32)
        part = part.astype(dq_part.dtype)
        dq_part[2 * t] = part[:, :ROWS]
        dq_part[2 * t + 1] = part[:, ROWS:]

    loop(0, PARTS, query_side)

    def send_dq(n):
        where, slot = query_peer(n)
        remote(dq_part.at[slot], dq_took.at[n - 1], send_sem.at[4], recv_sem.at[8], where).start()

    each(1, 8, send_dq)

    conclude(1)
    wait_for(dq_took, recv_sem.at[8])
    dq = dq_part[own].astype(jnp.float32)
    for n in range(7):
        dq += dq_took[n].astype(jnp.float32)
    grads[0] = dq.T.astype(jnp.bfloat16)

    conclude(0)
    for which in (1, 0):
        wait_for(pieces.at[which, pl.ds(1, 7)], recv_sem.at[11 + which])
        for n in range(8):
            fl, fc = yls[(YL - n // 2) % YL], cs[n % 2]
            first = lax.rem(fl, 2) * SPAN + fc * HALF + lax.div(fl, 2) * 16
            grads[1 + which, pl.ds(pl.multiple_of(first, 16), 16)] = pieces[which, n]

    pl.when(c == 0)(lambda: wait_for(kbuf.at[0, :, pl.ds(0, 448)], send_sem.at[0]))
    pl.when(c == 1)(lambda: wait_for(kbuf.at[0], send_sem.at[0]))
    wait_for(qbuf.at[:, pl.ds(ROWS, 7 * ROWS)], send_sem.at[1])
    wait_for(kbuf.at[0], swap_sem.at[4])
    wait_for(logs.at[pl.ds(1, 7)], send_sem.at[2])
    wait_for(deltas.at[pl.ds(1, 7)], send_sem.at[7])
    wait_for(give, send_sem.at[3])
    wait_for(dq_took, send_sem.at[4])
    wait_for(gathered, send_sem.at[5])
    wait_for(pieces.at[:, pl.ds(1, 7)], send_sem.at[6])


def local(queries, keys, values, grad_out, order, segment):
    bf16, f32, i32 = jnp.bfloat16, jnp.float32, jnp.int32
    vmem, hbm = pl.BlockSpec(memory_space=pltpu.VMEM), pl.BlockSpec(memory_space=pltpu.HBM)
    grads = pl.pallas_call(
        kernel,
        out_shape=pltpu.VMEM((3, ROWS, WIDTH), bf16),
        in_specs=[hbm] * 6,
        out_specs=vmem,
        scratch_shapes=[
            pltpu.SMEM((TOKENS // SPAN,), i32),
            pltpu.VMEM((TOKENS // WIDTH, WIDTH), i32),
            pltpu.VMEM((2, TILE, WIDTH), bf16),
            pltpu.VMEM((2, 2, 2, HALF, WIDTH), bf16),
            pltpu.VMEM((2, 2, TILE // 2, WIDTH), bf16),
            pltpu.VMEM((PARTS, TILE, LANES), f32),
            pltpu.VMEM((PARTS, TILE, LANES), f32),
            pltpu.VMEM((2, PARTS, TILE, LANES), bf16),
            pltpu.VMEM((PARTS, 8, LANES), f32),
            pltpu.VMEM((PARTS, 1, LANES), f32),
            pltpu.VMEM((PARTS, 8, LANES), f32),
            pltpu.VMEM((PARTS, 8, LANES), i32),
            pltpu.VMEM((PARTS, 8, LANES), i32),
            pltpu.VMEM((8, PARTS, 1, LANES), f32),
            pltpu.VMEM((8, PARTS, 1, LANES), f32),
            pltpu.VMEM((2, TILE // 2, WIDTH), bf16),
            pltpu.VMEM((2, TILE // 2, WIDTH), bf16),
            pltpu.VMEM((2, TILE // 2, WIDTH), bf16),
            pltpu.VMEM((2, 31, 16, WIDTH), bf16),
            pltpu.VMEM((2, 8, 16, WIDTH), bf16),
            pltpu.VMEM((8, WIDTH, ROWS), bf16),
            pltpu.VMEM((7, WIDTH, ROWS), bf16),
            pltpu.SemaphoreType.DMA((6,)),
            pltpu.SemaphoreType.DMA((8,)),
            pltpu.SemaphoreType.DMA((13,)),
            pltpu.SemaphoreType.DMA((5,)),
            pltpu.SemaphoreType.DMA((4,)),
        ],
        compiler_params=pltpu.CompilerParams(
            collective_id=0, has_side_effects=True, vmem_limit_bytes=55 << 20
        ),
        name="attention_backward",
    )(
        order,
        segment.reshape(-1, WIDTH),
        queries,
        keys.reshape(2, 2, HALF, WIDTH),
        values.reshape(2, 2, HALF, WIDTH),
        grad_out,
    )
    return grads[0:1], grads[1], grads[2]


def solution(mesh):
    placed = (
        P("head", "ctx", None),
        P("ctx", None),
        P("ctx", None),
        P("head", "ctx", None),
        P(),
        P(),
    )
    return jax.shard_map(
        local,
        mesh=mesh,
        in_specs=placed,
        out_specs=(P("head", "ctx", None), P("ctx", None), P("ctx", None)),
        check_vma=False,
    )
```

```python
import functools
import math

import jax
import jax.numpy as jnp
from jax import lax
from jax.experimental import pallas as pl
from jax.experimental.pallas import tpu as pltpu
from jax.sharding import PartitionSpec as P

YH, Z, X, YL, CORES = 2, 8, 4, 4, 2
DOCS = 6
TOKENS = 8192
SPAN = 64
HALF = SPAN // 2
ROWS = 2 * SPAN
WIDTH = 128
TILE = 1024
LANES = 256
PARTS = TILE // LANES
CHUNK = 128
NEGATIVE = -1e30
FLOOR = -1e20
MESH = pl.DeviceIdType.MESH
SCALE = 1.0 / math.sqrt(WIDTH)
LOG2E = 1.4426950408889634
NT = (((1,), (1,)), ((), ()))
TN = (((0,), (0,)), ((), ()))


def device(yh, z, x, yl, c):
    return {"ctx": yh * (Z * X) + z * X + x, "head": yl * CORES + c}


def kernel(
    order_in, segment_in, q_in, k_in, v_in, go_in, grads,
    places, docs, qbuf, kv, kbuf, scores, dprobs, pair, peaks, shares, weights, lows, highs,
    logs, deltas, give, take, total, gathered, pieces, dq_part, dq_took,
    local_sem, send_sem, recv_sem, swap_sem, take_sem,
):
    i, h = lax.axis_index("ctx"), lax.axis_index("head")
    yh, z, x = lax.div(i, Z * X), lax.rem(lax.div(i, X), Z), lax.rem(i, X)
    yl, c = lax.div(h, CORES), lax.rem(h, CORES)
    yp, yj = lax.rem(yl, 2), lax.div(yl, 2)
    own = yp * X + x
    zs = [lax.rem(z + n, Z) for n in range(Z)]
    xs = [lax.rem(x + n, X) for n in range(X)]
    yls = [lax.rem(yl + n, YL) for n in range(YL)]
    yps, yjs, yhs, cs = (yp, 1 - yp), (yj, 1 - yj), (yh, 1 - yh), (c, 1 - c)
    sibling = device(yh, z, x, yl, 1 - c)

    def query_peer(n):
        tx, tp = xs[n % X], yps[n // X]
        return device(yh, z, tx, yj * 2 + tp, c), tp * X + tx

    def near_peer(n):
        return device(yh, zs[n], x, yl, c)

    def far_peer(n):
        return device(1 - yh, zs[n], x, YL - 1 - yl, c)

    def owner(n):
        g, dz, jj = n // 16, n // 2 % 4 * 2 + n // 8 % 2, n % 2
        where = device(yhs[g], zs[(Z - dz) % Z], x, yjs[jj] * 2 + yp, c)
        return where, n // 2 * HALF + yjs[jj] * 16

    def head_peer(n):
        return device(yh, z, x, yls[n // 2], cs[n % 2])

    def remote(src, dst, send, recv, where):
        return pltpu.make_async_remote_copy(
            src_ref=src, dst_ref=dst, send_sem=send, recv_sem=recv,
            device_id=where, device_id_type=MESH,
        )

    def wait_for(ref, sem):
        pltpu.make_async_copy(ref, ref, sem).wait()

    def loop(first, last, body):
        def step(n, carry):
            body(n)
            return carry

        lax.fori_loop(first, last, step, 0)

    def each(first, last, body):
        for n in range(first, last):
            body(n)

    mine = pl.ds(pl.multiple_of(own * ROWS, ROWS), ROWS)
    loads = [
        pltpu.make_async_copy(k_in, kv.at[0], local_sem.at[0]),
        pltpu.make_async_copy(v_in, kv.at[1], local_sem.at[1]),
        pltpu.make_async_copy(q_in.at[0], qbuf.at[0, mine], local_sem.at[2]),
        pltpu.make_async_copy(go_in.at[0], qbuf.at[1, mine], local_sem.at[3]),
        pltpu.make_async_copy(order_in, places, local_sem.at[4]),
        pltpu.make_async_copy(segment_in, docs, local_sem.at[5]),
    ]
    for copy in loads:
        copy.start()

    barrier = pltpu.get_barrier_semaphore()

    def greet(where):
        pl.semaphore_signal(barrier, inc=1, device_id=where, device_id_type=MESH)

    each(1, 32, lambda n: greet(owner(n)[0]))
    each(0, 8, lambda n: greet(far_peer(n)))
    each(1, 8, lambda n: greet(query_peer(n)[0]))
    each(1, 8, lambda n: greet(head_peer(n)))

    for copy in loads:
        copy.wait()
    pl.semaphore_wait(barrier, 31 + 8 + 7 + 7)

    def send_far(a, m):
        rows = pl.ds(pl.multiple_of(256 + c * 128 + m * HALF, HALF), HALF)
        where = device(1 - yh, lax.rem(z + 2 * m + c, Z), x, YL - 1 - yl, c)
        remote(kv.at[a, 1 - yp], kbuf.at[a, :, rows], send_sem.at[0], recv_sem.at[2 * a + 1], where).start()

    def send_near(a, m):
        rows = pl.ds(pl.multiple_of(c * 128 + m * HALF, HALF), HALF)
        where = device(yh, lax.rem(z + 2 * m + c, Z), x, yl, c)

        def send():
            remote(kv.at[a, yp], kbuf.at[a, :, rows], send_sem.at[0], recv_sem.at[2 * a], where).start()

        if m > 0:
            send()
            return
        pl.when(c == 1)(send)

        @pl.when(c == 0)
        def _():
            pltpu.make_async_copy(kv.at[a, yp], kbuf.at[a, :, pl.ds(0, HALF)], recv_sem.at[2 * a]).start()

    def send_query(a, n):
        remote(
            qbuf.at[a, mine], qbuf.at[a, mine], send_sem.at[1], recv_sem.at[4 + a], query_peer(n)[0]
        ).start()

    for a in range(2):
        for m in range(4):
            send_near(a, m)
        for m in range(4):
            send_far(a, m)
        for n in range(1, 8):
            send_query(a, n)

    doc = docs[...]
    starts = [
        jnp.sum((doc < d).astype(jnp.int32), axis=(0, 1), keepdims=True) for d in range(1, DOCS)
    ]
    lane = lax.broadcasted_iota(jnp.int32, (8, ROWS), 1)
    for s in range(X):
        ctx = yh * (Z * X) + z * X + s
        first, second = places[2 * ctx], places[2 * ctx + 1]
        place = jnp.where(lane < SPAN, first * SPAN + lane, second * SPAN + lane - SPAN)
        low = jnp.zeros_like(place)
        for start in starts:
            low = jnp.maximum(low, jnp.where(start <= place, start, 0))
        for t in (s, s + X):
            lows[t // 2, :, (t % 2) * ROWS : (t % 2 + 1) * ROWS] = low
            highs[t // 2, :, (t % 2) * ROWS : (t % 2 + 1) * ROWS] = place

    def hand_over(a, g):
        rows = pl.ds(pl.multiple_of(g * 256 + c * 128, 128), 128)
        block = kbuf.at[a, :, rows]
        wait_for(block, recv_sem.at[2 * a + g])
        remote(block, block, swap_sem.at[4], swap_sem.at[2 * a + g], sibling).start()

    def handed(a, g):
        rows = pl.ds(pl.multiple_of(g * 256 + (1 - c) * 128, 128), 128)
        wait_for(kbuf.at[a, :, rows], swap_sem.at[2 * a + g])

    row = lax.broadcasted_iota(jnp.int32, (HALF, LANES), 0)

    def product(g, t):
        rows = pl.ds(pl.multiple_of(t * LANES, LANES), LANES)
        low, high = lows[t, 0:1, :], highs[t, 0:1, :]
        peak = None
        for b in range(2):
            s = lax.dot_general(
                kbuf[0, b, g * 256 : g * 256 + 256], qbuf[0, rows], NT, preferred_element_type=jnp.float32
            )
            for n in range(8):
                behind = zs[(Z - (n % 4 * 2 + n // 4)) % Z]
                ctx = yhs[g] * (Z * X) + behind * X + x
                place = places[2 * ctx + yp] * SPAN + b * HALF + row
                masked = jnp.where(
                    (place >= low) & (place <= high), s[n * HALF : n * HALF + HALF], NEGATIVE
                )
                first = b * 512 + g * 256 + n * HALF
                scores[t, first : first + HALF] = masked
                top = jnp.max(masked.reshape(HALF // 8, 8, LANES), axis=0)
                peak = top if peak is None else jnp.maximum(peak, top)
        peaks[g, t] = peak

    def weigh(g, t):
        peak = jnp.maximum(jnp.max(peaks[g, t], axis=0, keepdims=True), FLOOR)

        def step(n, carry):
            first = lax.div(n, 2) * 512 + g * 256 + lax.rem(n, 2) * CHUNK
            rows = pl.ds(pl.multiple_of(first, CHUNK), CHUNK)
            expo = jnp.exp2((scores[t, rows] - peak) * (SCALE * LOG2E))
            scores[t, rows] = expo
            return carry + jnp.sum(expo.reshape(CHUNK // 8, 8, LANES), axis=0)

        mass = lax.fori_loop(0, 4, step, jnp.zeros((8, LANES), jnp.float32))
        mass = jnp.sum(mass, axis=0, keepdims=True)
        peak = peak * (SCALE * LOG2E)
        peaks[g, t, 0:1] = peak
        if g == 0:
            shares[0, t] = mass
            return
        peak_near = peaks[0, t, 0:1]
        top = jnp.maximum(peak_near, peak)
        near, far = jnp.exp2(peak_near - top), jnp.exp2(peak - top)
        mass = jnp.maximum(near * shares[0, t] + far * mass, 1e-30)
        shares[0, t] = near / mass
        shares[1, t] = far / mass
        logs[0, t] = top + jnp.log2(mass)

    def send_logs(n):
        remote(logs.at[0], logs.at[n], send_sem.at[2], recv_sem.at[6], query_peer(n)[0]).start()

    def cotangent(g, t):
        rows = pl.ds(pl.multiple_of(t * LANES, LANES), LANES)
        weighted = jnp.zeros((8, LANES), jnp.float32)
        for b in range(2):
            keys = slice(b * 512 + g * 256, b * 512 + g * 256 + 256)
            d = lax.dot_general(
                kbuf[1, b, g * 256 : g * 256 + 256], qbuf[1, rows], NT, preferred_element_type=jnp.float32
            )
            dprobs[t, keys] = d
            weighted += jnp.sum((scores[t, keys] * d).reshape(32, 8, LANES), axis=0)
        weighted = jnp.sum(weighted, axis=0, keepdims=True)
        if g == 0:
            weights[t] = weighted
        else:
            deltas[0, t] = weights[t] * shares[0, t] + weighted * shares[1, t]

    hand_over(0, 0)
    wait_for(qbuf.at[0, pl.ds(ROWS, 7 * ROWS)], recv_sem.at[4])
    handed(0, 0)
    loop(0, PARTS, functools.partial(product, 0))
    loop(0, PARTS, functools.partial(weigh, 0))
    hand_over(0, 1)
    hand_over(1, 0)
    handed(0, 1)
    loop(0, PARTS, functools.partial(product, 1))
    loop(0, PARTS, functools.partial(weigh, 1))
    each(1, 8, send_logs)
    hand_over(1, 1)
    wait_for(qbuf.at[1, pl.ds(ROWS, 7 * ROWS)], recv_sem.at[5])
    handed(1, 0)
    loop(0, PARTS, functools.partial(cotangent, 0))
    handed(1, 1)
    loop(0, PARTS, functools.partial(cotangent, 1))

    def send_deltas(n):
        remote(deltas.at[0], deltas.at[n], send_sem.at[7], recv_sem.at[7], query_peer(n)[0]).start()

    each(1, 8, send_deltas)

    def lse_of(t):
        every = [logs[n, t] for n in range(8)]
        top = functools.reduce(jnp.maximum, every)
        parts = [jnp.exp2(e - top) for e in every]
        return top, parts, functools.reduce(jnp.add, parts)

    def normalize(t):
        top, _, mass = lse_of(t)
        for g in range(2):
            peaks[g, t, 0:1] = jnp.exp2(peaks[g, t, 0:1] - top) / mass

    def center(t):
        _, parts, mass = lse_of(t)
        peaks[0, t, 1:2] = functools.reduce(jnp.add, [s * deltas[n, t] for n, s in enumerate(parts)]) / mass

    def value_weights(first, g):
        def step(n):
            t, rows = lax.div(n, 2), pl.ds(pl.multiple_of(first + lax.rem(n, 2) * CHUNK, CHUNK), CHUNK)
            pair[1, t, rows] = (scores[t, rows] * peaks[g, t, 0:1]).astype(jnp.bfloat16)

        loop(0, 2 * PARTS, step)

    def key_weights(first, g):
        def step(n):
            t, rows = lax.div(n, 2), pl.ds(pl.multiple_of(first + lax.rem(n, 2) * CHUNK, CHUNK), CHUNK)
            probs = scores[t, rows] * peaks[g, t, 0:1]
            pair[0, t, rows] = (probs * (dprobs[t, rows] - peaks[0, t, 1:2]) * SCALE).astype(jnp.bfloat16)

        loop(0, 2 * PARTS, step)

    def key_side(which, first):
        acc = jnp.zeros((LANES, WIDTH), jnp.float32)
        for t in range(PARTS):
            acc += jnp.dot(
                pair[which, t, pl.ds(first, LANES)], qbuf[which, t * LANES : t * LANES + LANES],
                preferred_element_type=jnp.float32,
            )
        return acc

    def send_piece(which, n):
        where, first = owner(n)
        rows = pl.ds(pl.multiple_of(first, 16), 16)
        remote(
            total.at[which, rows], gathered.at[which, n - 1],
            send_sem.at[5], recv_sem.at[9 + which], where,
        ).start()

    def one_side(which, weigh_chunk):
        for r in (1, 0):
            first = pl.multiple_of((1 - c) * 512 + r * LANES, LANES)
            rows = pl.ds(r * LANES, LANES)
            weigh_chunk(first, r)
            give[which, rows] = key_side(which, first).astype(jnp.bfloat16)
            remote(
                give.at[which, rows], take.at[which, rows],
                send_sem.at[3], take_sem.at[2 * which + r], sibling,
            ).start()
        for r in (1, 0):
            first = pl.multiple_of(c * 512 + r * LANES, LANES)
            rows = pl.ds(r * LANES, LANES)
            weigh_chunk(first, r)
            acc = key_side(which, first)
            wait_for(take.at[which, rows], take_sem.at[2 * which + r])
            total[which, rows] = (acc + take[which, rows].astype(jnp.float32)).astype(jnp.bfloat16)
            each(max(1, 16 * r), 16 * r + 16, functools.partial(send_piece, which))

    def conclude(which):
        wait_for(gathered.at[which], recv_sem.at[9 + which])
        result = total[which, pl.ds(pl.multiple_of(yj * 16, 16), 16)].astype(jnp.float32)
        for n in range(31):
            result += gathered[which, n].astype(jnp.float32)
        pieces[which, 0] = result.astype(jnp.bfloat16)
        for n in range(1, 8):
            remote(
                pieces.at[which, 0], pieces.at[which, n],
                send_sem.at[6], recv_sem.at[11 + which], head_peer(n),
            ).start()

    wait_for(logs.at[pl.ds(1, 7)], recv_sem.at[6])
    loop(0, PARTS, normalize)
    one_side(1, value_weights)
    wait_for(deltas.at[pl.ds(1, 7)], recv_sem.at[7])
    loop(0, PARTS, center)
    one_side(0, key_weights)

    def query_side(t):
        keys = kbuf[0].reshape(TILE, WIDTH)
        part = lax.dot_general(keys, pair[0, t], TN, preferred_element_type=jnp.float32)
        part = part.astype(dq_part.dtype)
        dq_part[2 * t] = part[:, :ROWS]
        dq_part[2 * t + 1] = part[:, ROWS:]

    loop(0, PARTS, query_side)

    def send_dq(n):
        where, slot = query_peer(n)
        remote(dq_part.at[slot], dq_took.at[n - 1], send_sem.at[4], recv_sem.at[8], where).start()

    each(1, 8, send_dq)

    conclude(1)
    wait_for(dq_took, recv_sem.at[8])
    dq = dq_part[own].astype(jnp.float32)
    for n in range(7):
        dq += dq_took[n].astype(jnp.float32)
    grads[0] = dq.T.astype(jnp.bfloat16)

    conclude(0)
    for which in (1, 0):
        wait_for(pieces.at[which, pl.ds(1, 7)], recv_sem.at[11 + which])
        for n in range(8):
            fl, fc = yls[(YL - n // 2) % YL], cs[n % 2]
            first = lax.rem(fl, 2) * SPAN + fc * HALF + lax.div(fl, 2) * 16
            grads[1 + which, pl.ds(pl.multiple_of(first, 16), 16)] = pieces[which, n]

    pl.when(c == 0)(lambda: wait_for(kbuf.at[0, :, pl.ds(0, 448)], send_sem.at[0]))
    pl.when(c == 1)(lambda: wait_for(kbuf.at[0], send_sem.at[0]))
    wait_for(qbuf.at[:, pl.ds(ROWS, 7 * ROWS)], send_sem.at[1])
    wait_for(kbuf.at[0], swap_sem.at[4])
    wait_for(logs.at[pl.ds(1, 7)], send_sem.at[2])
    wait_for(deltas.at[pl.ds(1, 7)], send_sem.at[7])
    wait_for(give, send_sem.at[3])
    wait_for(dq_took, send_sem.at[4])
    wait_for(gathered, send_sem.at[5])
    wait_for(pieces.at[:, pl.ds(1, 7)], send_sem.at[6])


def local(queries, keys, values, grad_out, order, segment):
    bf16, f32, i32 = jnp.bfloat16, jnp.float32, jnp.int32
    vmem, hbm = pl.BlockSpec(memory_space=pltpu.VMEM), pl.BlockSpec(memory_space=pltpu.HBM)
    grads = pl.pallas_call(
        kernel,
        out_shape=pltpu.VMEM((3, ROWS, WIDTH), bf16),
        in_specs=[hbm] * 6,
        out_specs=vmem,
        scratch_shapes=[
            pltpu.SMEM((TOKENS // SPAN,), i32),
            pltpu.VMEM((TOKENS // WIDTH, WIDTH), i32),
            pltpu.VMEM((2, TILE, WIDTH), bf16),
            pltpu.VMEM((2, 2, 2, HALF, WIDTH), bf16),
            pltpu.VMEM((2, 2, TILE // 2, WIDTH), bf16),
            pltpu.VMEM((PARTS, TILE, LANES), f32),
            pltpu.VMEM((PARTS, TILE, LANES), f32),
            pltpu.VMEM((2, PARTS, TILE, LANES), bf16),
            pltpu.VMEM((2, PARTS, 8, LANES), f32),
            pltpu.VMEM((2, PARTS, 1, LANES), f32),
            pltpu.VMEM((PARTS, 1, LANES), f32),
            pltpu.VMEM((PARTS, 8, LANES), i32),
            pltpu.VMEM((PARTS, 8, LANES), i32),
            pltpu.VMEM((8, PARTS, 1, LANES), f32),
            pltpu.VMEM((8, PARTS, 1, LANES), f32),
            pltpu.VMEM((2, TILE // 2, WIDTH), bf16),
            pltpu.VMEM((2, TILE // 2, WIDTH), bf16),
            pltpu.VMEM((2, TILE // 2, WIDTH), bf16),
            pltpu.VMEM((2, 31, 16, WIDTH), bf16),
            pltpu.VMEM((2, 8, 16, WIDTH), bf16),
            pltpu.VMEM((8, WIDTH, ROWS), bf16),
            pltpu.VMEM((7, WIDTH, ROWS), bf16),
            pltpu.SemaphoreType.DMA((6,)),
            pltpu.SemaphoreType.DMA((8,)),
            pltpu.SemaphoreType.DMA((13,)),
            pltpu.SemaphoreType.DMA((5,)),
            pltpu.SemaphoreType.DMA((4,)),
        ],
        compiler_params=pltpu.CompilerParams(
            collective_id=0, has_side_effects=True, vmem_limit_bytes=55 << 20
        ),
        name="attention_backward",
    )(
        order,
        segment.reshape(-1, WIDTH),
        queries,
        keys.reshape(2, 2, HALF, WIDTH),
        values.reshape(2, 2, HALF, WIDTH),
        grad_out,
    )
    return grads[0:1], grads[1], grads[2]


def solution(mesh):
    placed = (
        P("head", "ctx", None),
        P("ctx", None),
        P("ctx", None),
        P("head", "ctx", None),
        P(),
        P(),
    )
    return jax.shard_map(
        local,
        mesh=mesh,
        in_specs=placed,
        out_specs=(P("head", "ctx", None), P("ctx", None), P("ctx", None)),
        check_vma=False,
    )
```

```python
import functools
import math

import jax
import jax.numpy as jnp
from jax import lax
from jax.experimental import pallas as pl
from jax.experimental.pallas import tpu as pltpu
from jax.sharding import PartitionSpec as P

YH, Z, X, YL, CORES = 2, 8, 4, 4, 2
DOCS = 6
TOKENS = 8192
SPAN = 64
HALF = SPAN // 2
ROWS = 2 * SPAN
WIDTH = 128
TILE = 1024
LANES = 256
PARTS = TILE // LANES
CHUNK = 128
NEGATIVE = -1e30
FLOOR = -1e20
MESH = pl.DeviceIdType.MESH
SCALE = 1.0 / math.sqrt(WIDTH)
LOG2E = 1.4426950408889634
NT = (((1,), (1,)), ((), ()))
TN = (((0,), (0,)), ((), ()))


def device(yh, z, x, yl, c):
    return {"ctx": yh * (Z * X) + z * X + x, "head": yl * CORES + c}


def kernel(
    order_in, segment_in, q_in, k_in, v_in, go_in, grads,
    places, docs, qbuf, kv, mirrored, kbuf, scores, dprobs, pair, peaks, shares, weights, lows, highs,
    logs, deltas, give, take, total, gathered, pieces, dq_part, dq_took,
    local_sem, send_sem, recv_sem, swap_sem, take_sem,
):
    i, h = lax.axis_index("ctx"), lax.axis_index("head")
    yh, z, x = lax.div(i, Z * X), lax.rem(lax.div(i, X), Z), lax.rem(i, X)
    yl, c = lax.div(h, CORES), lax.rem(h, CORES)
    yp, yj = lax.rem(yl, 2), lax.div(yl, 2)
    own = yp * X + x
    zs = [lax.rem(z + n, Z) for n in range(Z)]
    xs = [lax.rem(x + n, X) for n in range(X)]
    yls = [lax.rem(yl + n, YL) for n in range(YL)]
    yps, yjs, yhs, cs = (yp, 1 - yp), (yj, 1 - yj), (yh, 1 - yh), (c, 1 - c)
    sibling = device(yh, z, x, yl, 1 - c)

    def query_peer(n):
        tx, tp = xs[n % X], yps[n // X]
        return device(yh, z, tx, yj * 2 + tp, c), tp * X + tx

    def near_peer(n):
        return device(yh, zs[n], x, yl, c)

    mirror = device(1 - yh, z, x, YL - 1 - yl, c)

    def line_peer(n):
        q = lax.rem(yh * 2 + yj + n // 2, 4)
        return device(lax.div(q, 2), z, x, lax.rem(q, 2) * 2 + yp, cs[n % 2])

    def owner(n):
        g, dz, jj = n // 16, n // 2 % 4 * 2 + n // 8 % 2, n % 2
        where = device(yhs[g], zs[(Z - dz) % Z], x, yjs[jj] * 2 + yp, c)
        return where, n // 2 * HALF + yjs[jj] * 16

    def head_peer(n):
        return device(yh, z, x, yls[n // 2], cs[n % 2])

    def remote(src, dst, send, recv, where):
        return pltpu.make_async_remote_copy(
            src_ref=src, dst_ref=dst, send_sem=send, recv_sem=recv,
            device_id=where, device_id_type=MESH,
        )

    def wait_for(ref, sem):
        pltpu.make_async_copy(ref, ref, sem).wait()

    def loop(first, last, body):
        def step(n, carry):
            body(n)
            return carry

        lax.fori_loop(first, last, step, 0)

    def each(first, last, body):
        for n in range(first, last):
            body(n)

    mine = pl.ds(pl.multiple_of(own * ROWS, ROWS), ROWS)
    loads = [
        pltpu.make_async_copy(k_in, kv.at[0], local_sem.at[0]),
        pltpu.make_async_copy(v_in, kv.at[1], local_sem.at[1]),
        pltpu.make_async_copy(q_in.at[0], qbuf.at[0, mine], local_sem.at[2]),
        pltpu.make_async_copy(go_in.at[0], qbuf.at[1, mine], local_sem.at[3]),
        pltpu.make_async_copy(order_in, places, local_sem.at[4]),
        pltpu.make_async_copy(segment_in, docs, local_sem.at[5]),
    ]
    for copy in loads:
        copy.start()

    barrier = pltpu.get_barrier_semaphore()

    def greet(where):
        pl.semaphore_signal(barrier, inc=1, device_id=where, device_id_type=MESH)

    each(2, 8, lambda n: greet(line_peer(n)))
    each(1, 8, lambda n: greet(near_peer(n)))
    greet(mirror)
    each(1, 8, lambda n: greet(query_peer(n)[0]))
    each(1, 8, lambda n: greet(head_peer(n)))

    for copy in loads:
        copy.wait()
    pl.semaphore_wait(barrier, 6 + 7 + 1 + 7 + 7)

    def send_mirror(a):
        remote(kv.at[a, 1 - yp], mirrored.at[a], send_sem.at[8], recv_sem.at[13 + a], mirror).start()

    def send_along(block, a, g, m):
        rows = pl.ds(pl.multiple_of(g * 256 + c * 128 + m * HALF, HALF), HALF)
        where = device(yh, lax.rem(z + 2 * m + c, Z), x, yl, c)

        def send():
            remote(block, kbuf.at[a, :, rows], send_sem.at[0], recv_sem.at[2 * a + g], where).start()

        if m > 0:
            send()
            return
        pl.when(c == 1)(send)

        @pl.when(c == 0)
        def _():
            slot = kbuf.at[a, :, pl.ds(g * 256, HALF)]
            pltpu.make_async_copy(block, slot, recv_sem.at[2 * a + g]).start()

    def send_query(a, n):
        remote(
            qbuf.at[a, mine], qbuf.at[a, mine], send_sem.at[1], recv_sem.at[4 + a], query_peer(n)[0]
        ).start()

    send_mirror(0)
    send_mirror(1)
    for a in range(2):
        for m in range(4):
            send_along(kv.at[a, yp], a, 0, m)
        for n in range(1, 8):
            send_query(a, n)

    doc = docs[...]
    starts = [
        jnp.sum((doc < d).astype(jnp.int32), axis=(0, 1), keepdims=True) for d in range(1, DOCS)
    ]
    lane = lax.broadcasted_iota(jnp.int32, (8, ROWS), 1)
    for s in range(X):
        ctx = yh * (Z * X) + z * X + s
        first, second = places[2 * ctx], places[2 * ctx + 1]
        place = jnp.where(lane < SPAN, first * SPAN + lane, second * SPAN + lane - SPAN)
        low = jnp.zeros_like(place)
        for start in starts:
            low = jnp.maximum(low, jnp.where(start <= place, start, 0))
        for t in (s, s + X):
            lows[t // 2, :, (t % 2) * ROWS : (t % 2 + 1) * ROWS] = low
            highs[t // 2, :, (t % 2) * ROWS : (t % 2 + 1) * ROWS] = place

    def hand_over(a, g):
        rows = pl.ds(pl.multiple_of(g * 256 + c * 128, 128), 128)
        block = kbuf.at[a, :, rows]
        wait_for(block, recv_sem.at[2 * a + g])
        remote(block, block, swap_sem.at[4], swap_sem.at[2 * a + g], sibling).start()

    def handed(a, g):
        rows = pl.ds(pl.multiple_of(g * 256 + (1 - c) * 128, 128), 128)
        wait_for(kbuf.at[a, :, rows], swap_sem.at[2 * a + g])

    row = lax.broadcasted_iota(jnp.int32, (HALF, LANES), 0)

    def product(g, t):
        rows = pl.ds(pl.multiple_of(t * LANES, LANES), LANES)
        low, high = lows[t, 0:1, :], highs[t, 0:1, :]
        peak = None
        for b in range(2):
            s = lax.dot_general(
                kbuf[0, b, g * 256 : g * 256 + 256], qbuf[0, rows], NT, preferred_element_type=jnp.float32
            )
            for n in range(8):
                behind = zs[(Z - (n % 4 * 2 + n // 4)) % Z]
                ctx = yhs[g] * (Z * X) + behind * X + x
                place = places[2 * ctx + yp] * SPAN + b * HALF + row
                masked = jnp.where(
                    (place >= low) & (place <= high), s[n * HALF : n * HALF + HALF], NEGATIVE
                )
                first = b * 512 + g * 256 + n * HALF
                scores[t, first : first + HALF] = masked
                top = jnp.max(masked.reshape(HALF // 8, 8, LANES), axis=0)
                peak = top if peak is None else jnp.maximum(peak, top)
        peaks[g, t] = peak

    def weigh(g, t):
        peak = jnp.maximum(jnp.max(peaks[g, t], axis=0, keepdims=True), FLOOR)

        def step(n, carry):
            first = lax.div(n, 2) * 512 + g * 256 + lax.rem(n, 2) * CHUNK
            rows = pl.ds(pl.multiple_of(first, CHUNK), CHUNK)
            expo = jnp.exp2((scores[t, rows] - peak) * (SCALE * LOG2E))
            scores[t, rows] = expo
            return carry + jnp.sum(expo.reshape(CHUNK // 8, 8, LANES), axis=0)

        mass = lax.fori_loop(0, 4, step, jnp.zeros((8, LANES), jnp.float32))
        mass = jnp.sum(mass, axis=0, keepdims=True)
        peak = peak * (SCALE * LOG2E)
        peaks[g, t, 0:1] = peak
        if g == 0:
            shares[0, t] = mass
            return
        peak_near = peaks[0, t, 0:1]
        top = jnp.maximum(peak_near, peak)
        near, far = jnp.exp2(peak_near - top), jnp.exp2(peak - top)
        mass = jnp.maximum(near * shares[0, t] + far * mass, 1e-30)
        shares[0, t] = near / mass
        shares[1, t] = far / mass
        logs[0, t] = top + jnp.log2(mass)

    def send_logs(n):
        remote(logs.at[0], logs.at[n], send_sem.at[2], recv_sem.at[6], query_peer(n)[0]).start()

    def cotangent(g, t):
        rows = pl.ds(pl.multiple_of(t * LANES, LANES), LANES)
        weighted = jnp.zeros((8, LANES), jnp.float32)
        for b in range(2):
            keys = slice(b * 512 + g * 256, b * 512 + g * 256 + 256)
            d = lax.dot_general(
                kbuf[1, b, g * 256 : g * 256 + 256], qbuf[1, rows], NT, preferred_element_type=jnp.float32
            )
            dprobs[t, keys] = d
            weighted += jnp.sum((scores[t, keys] * d).reshape(32, 8, LANES), axis=0)
        weighted = jnp.sum(weighted, axis=0, keepdims=True)
        if g == 0:
            weights[t] = weighted
        else:
            deltas[0, t] = weights[t] * shares[0, t] + weighted * shares[1, t]

    for a in range(2):
        wait_for(mirrored.at[a], recv_sem.at[13 + a])
        for m in range(4):
            send_along(mirrored.at[a], a, 1, m)
    hand_over(0, 0)
    wait_for(qbuf.at[0, pl.ds(ROWS, 7 * ROWS)], recv_sem.at[4])
    handed(0, 0)
    loop(0, PARTS, functools.partial(product, 0))
    hand_over(1, 0)
    loop(0, PARTS, functools.partial(weigh, 0))
    hand_over(0, 1)
    hand_over(1, 1)
    handed(0, 1)
    loop(0, PARTS, functools.partial(product, 1))
    loop(0, PARTS, functools.partial(weigh, 1))
    each(1, 8, send_logs)
    wait_for(qbuf.at[1, pl.ds(ROWS, 7 * ROWS)], recv_sem.at[5])
    handed(1, 0)
    loop(0, PARTS, functools.partial(cotangent, 0))
    handed(1, 1)
    loop(0, PARTS, functools.partial(cotangent, 1))

    def send_deltas(n):
        remote(deltas.at[0], deltas.at[n], send_sem.at[7], recv_sem.at[7], query_peer(n)[0]).start()

    each(1, 8, send_deltas)

    def lse_of(t):
        every = [logs[n, t] for n in range(8)]
        top = functools.reduce(jnp.maximum, every)
        parts = [jnp.exp2(e - top) for e in every]
        return top, parts, functools.reduce(jnp.add, parts)

    def normalize(t):
        top, _, mass = lse_of(t)
        for g in range(2):
            peaks[g, t, 0:1] = jnp.exp2(peaks[g, t, 0:1] - top) / mass

    def center(t):
        _, parts, mass = lse_of(t)
        peaks[0, t, 1:2] = functools.reduce(jnp.add, [s * deltas[n, t] for n, s in enumerate(parts)]) / mass

    def value_weights(first, g):
        def step(n):
            t, rows = lax.div(n, 2), pl.ds(pl.multiple_of(first + lax.rem(n, 2) * CHUNK, CHUNK), CHUNK)
            pair[1, t, rows] = (scores[t, rows] * peaks[g, t, 0:1]).astype(jnp.bfloat16)

        loop(0, 2 * PARTS, step)

    def key_weights(first, g):
        def step(n):
            t, rows = lax.div(n, 2), pl.ds(pl.multiple_of(first + lax.rem(n, 2) * CHUNK, CHUNK), CHUNK)
            probs = scores[t, rows] * peaks[g, t, 0:1]
            pair[0, t, rows] = (probs * (dprobs[t, rows] - peaks[0, t, 1:2]) * SCALE).astype(jnp.bfloat16)

        loop(0, 2 * PARTS, step)

    def key_side(which, first):
        acc = jnp.zeros((LANES, WIDTH), jnp.float32)
        for t in range(PARTS):
            acc += jnp.dot(
                pair[which, t, pl.ds(first, LANES)], qbuf[which, t * LANES : t * LANES + LANES],
                preferred_element_type=jnp.float32,
            )
        return acc

    def send_piece(which, n):
        where, first = owner(n)
        rows = pl.ds(pl.multiple_of(first, 16), 16)
        remote(
            total.at[which, rows], gathered.at[which, n - 1],
            send_sem.at[5], recv_sem.at[9 + which], where,
        ).start()

    def one_side(which, weigh_chunk):
        for r in (1, 0):
            first = pl.multiple_of((1 - c) * 512 + r * LANES, LANES)
            rows = pl.ds(r * LANES, LANES)
            weigh_chunk(first, r)
            give[which, rows] = key_side(which, first).astype(jnp.bfloat16)
            remote(
                give.at[which, rows], take.at[which, rows],
                send_sem.at[3], take_sem.at[2 * which + r], sibling,
            ).start()
        for r in (1, 0):
            first = pl.multiple_of(c * 512 + r * LANES, LANES)
            rows = pl.ds(r * LANES, LANES)
            weigh_chunk(first, r)
            acc = key_side(which, first)
            wait_for(take.at[which, rows], take_sem.at[2 * which + r])
            total[which, rows] = (acc + take[which, rows].astype(jnp.float32)).astype(jnp.bfloat16)
            each(max(1, 16 * r), 16 * r + 16, functools.partial(send_piece, which))

    def conclude(which):
        wait_for(gathered.at[which], recv_sem.at[9 + which])
        result = total[which, pl.ds(pl.multiple_of(yj * 16, 16), 16)].astype(jnp.float32)
        for n in range(31):
            result += gathered[which, n].astype(jnp.float32)
        pieces[which, 0] = result.astype(jnp.bfloat16)
        for n in range(1, 8):
            remote(
                pieces.at[which, 0], pieces.at[which, n],
                send_sem.at[6], recv_sem.at[11 + which], head_peer(n),
            ).start()

    wait_for(logs.at[pl.ds(1, 7)], recv_sem.at[6])
    loop(0, PARTS, normalize)
    one_side(1, value_weights)
    wait_for(deltas.at[pl.ds(1, 7)], recv_sem.at[7])
    loop(0, PARTS, center)
    one_side(0, key_weights)

    def query_side(t):
        keys = kbuf[0].reshape(TILE, WIDTH)
        part = lax.dot_general(keys, pair[0, t], TN, preferred_element_type=jnp.float32)
        part = part.astype(dq_part.dtype)
        dq_part[2 * t] = part[:, :ROWS]
        dq_part[2 * t + 1] = part[:, ROWS:]

    loop(0, PARTS, query_side)

    def send_dq(n):
        where, slot = query_peer(n)
        remote(dq_part.at[slot], dq_took.at[n - 1], send_sem.at[4], recv_sem.at[8], where).start()

    each(1, 8, send_dq)

    conclude(1)
    wait_for(dq_took, recv_sem.at[8])
    dq = dq_part[own].astype(jnp.float32)
    for n in range(7):
        dq += dq_took[n].astype(jnp.float32)
    grads[0] = dq.T.astype(jnp.bfloat16)

    conclude(0)
    for which in (1, 0):
        wait_for(pieces.at[which, pl.ds(1, 7)], recv_sem.at[11 + which])
        for n in range(8):
            fl, fc = yls[(YL - n // 2) % YL], cs[n % 2]
            first = lax.rem(fl, 2) * SPAN + fc * HALF + lax.div(fl, 2) * 16
            grads[1 + which, pl.ds(pl.multiple_of(first, 16), 16)] = pieces[which, n]

    wait_for(mirrored, send_sem.at[8])
    pl.when(c == 0)(lambda: wait_for(kbuf.at[0, :, pl.ds(0, 384)], send_sem.at[0]))
    pl.when(c == 1)(lambda: wait_for(kbuf.at[0], send_sem.at[0]))
    wait_for(qbuf.at[:, pl.ds(ROWS, 7 * ROWS)], send_sem.at[1])
    wait_for(kbuf.at[0], swap_sem.at[4])
    wait_for(logs.at[pl.ds(1, 7)], send_sem.at[2])
    wait_for(deltas.at[pl.ds(1, 7)], send_sem.at[7])
    wait_for(give, send_sem.at[3])
    wait_for(dq_took, send_sem.at[4])
    wait_for(gathered, send_sem.at[5])
    wait_for(pieces.at[:, pl.ds(1, 7)], send_sem.at[6])


def local(queries, keys, values, grad_out, order, segment):
    bf16, f32, i32 = jnp.bfloat16, jnp.float32, jnp.int32
    vmem, hbm = pl.BlockSpec(memory_space=pltpu.VMEM), pl.BlockSpec(memory_space=pltpu.HBM)
    grads = pl.pallas_call(
        kernel,
        out_shape=pltpu.VMEM((3, ROWS, WIDTH), bf16),
        in_specs=[hbm] * 6,
        out_specs=vmem,
        scratch_shapes=[
            pltpu.SMEM((TOKENS // SPAN,), i32),
            pltpu.VMEM((TOKENS // WIDTH, WIDTH), i32),
            pltpu.VMEM((2, TILE, WIDTH), bf16),
            pltpu.VMEM((2, 2, 2, HALF, WIDTH), bf16),
            pltpu.VMEM((2, 2, HALF, WIDTH), bf16),
            pltpu.VMEM((2, 2, TILE // 2, WIDTH), bf16),
            pltpu.VMEM((PARTS, TILE, LANES), f32),
            pltpu.VMEM((PARTS, TILE, LANES), f32),
            pltpu.VMEM((2, PARTS, TILE, LANES), bf16),
            pltpu.VMEM((2, PARTS, 8, LANES), f32),
            pltpu.VMEM((2, PARTS, 1, LANES), f32),
            pltpu.VMEM((PARTS, 1, LANES), f32),
            pltpu.VMEM((PARTS, 8, LANES), i32),
            pltpu.VMEM((PARTS, 8, LANES), i32),
            pltpu.VMEM((8, PARTS, 1, LANES), f32),
            pltpu.VMEM((8, PARTS, 1, LANES), f32),
            pltpu.VMEM((2, TILE // 2, WIDTH), bf16),
            pltpu.VMEM((2, TILE // 2, WIDTH), bf16),
            pltpu.VMEM((2, TILE // 2, WIDTH), bf16),
            pltpu.VMEM((2, 31, 16, WIDTH), bf16),
            pltpu.VMEM((2, 8, 16, WIDTH), bf16),
            pltpu.VMEM((8, WIDTH, ROWS), bf16),
            pltpu.VMEM((7, WIDTH, ROWS), bf16),
            pltpu.SemaphoreType.DMA((6,)),
            pltpu.SemaphoreType.DMA((9,)),
            pltpu.SemaphoreType.DMA((15,)),
            pltpu.SemaphoreType.DMA((5,)),
            pltpu.SemaphoreType.DMA((4,)),
        ],
        compiler_params=pltpu.CompilerParams(
            collective_id=0, has_side_effects=True, vmem_limit_bytes=55 << 20
        ),
        name="attention_backward",
    )(
        order,
        segment.reshape(-1, WIDTH),
        queries,
        keys.reshape(2, 2, HALF, WIDTH),
        values.reshape(2, 2, HALF, WIDTH),
        grad_out,
    )
    return grads[0:1], grads[1], grads[2]


def solution(mesh):
    placed = (
        P("head", "ctx", None),
        P("ctx", None),
        P("ctx", None),
        P("head", "ctx", None),
        P(),
        P(),
    )
    return jax.shard_map(
        local,
        mesh=mesh,
        in_specs=placed,
        out_specs=(P("head", "ctx", None), P("ctx", None), P("ctx", None)),
        check_vma=False,
    )
```
